256 devices in a mesh: ctx: 32 (over z, x_lo, core), head: 8 (over x_hi, y).
Axes of the slice: x: 4 (x_hi: 2, x_lo: 2; x = x_hi * 2 + x_lo), y: 4, z: 8, core: 2. Of those that a mesh axis runs over, the one named last changes fastest.
Arguments:
- queries: bfloat16 [32768, 3072], P(('ctx', 'head')), may hold values from -48 to 48
- key_rows: bfloat16 [32768, 3072], P(('ctx', 'head')), may hold values from -6 to 6
- value_rows: bfloat16 [32768, 3072], P(('ctx', 'head')), may hold values from -6 to 6
- out_cotangent: bfloat16 [32768, 3072], P(('ctx', 'head')), may hold values from -6 to 6
- gate_table: float32 [128, 3072], replicated, may hold values from -6 to 6
- span_ids: int32 [32768], replicated, may hold values from 0 to 191, never falling along the last dimension, each value on 1 to 256 neighbouring positions
- noise_level: int32 [192], replicated, may hold values from 0 to 127
- block_mask: int32 [192, 192], replicated, may hold values from 0 to 1, as said below
Outputs:
- mixed_out: bfloat16 [32768, 3072], P(('ctx', 'head'))
- query_grad: bfloat16 [32768, 3072], P(('ctx', 'head'))
- key_grad: bfloat16 [32768, 3072], P(('ctx', 'head'))
- value_grad: bfloat16 [32768, 3072], P(('ctx', 'head'))
- gate_grad: float32 [128, 3072], replicated
The draws below stay inside these ranges and needn't reach their ends.
Inputs may be any that keep to these rules, and one draw needn't show every extreme that they name: `span_ids`: span ids never fall along the tokens; every span holds 1 to 256 tokens, one span exactly 256. `block_mask`: entries are 0 or 1; entries [c, c] and [c, c - 1] are 1 for every span c.
All inputs are finite; a program needn't handle non-finite values.
Results may differ from the reference program's by a relative error of at most 0.023.
Values may be sent and summed in bfloat16 or wider, within the bound.
A program may use at most 128 MiB of HBM per device.

```python
import math
import jax
import jax.numpy as jnp
import numpy as np
from jax import lax

HEADS = 24
DH = 128
SPAN = 256
LEVELS = 128
TOKENS = 32768
WINDOW = 1024
SPANS = 192


def shared_rows(key):
    full_width = HEADS * DH
    normal_q = jax.random.normal(jax.random.fold_in(key, 101), (TOKENS, full_width), jnp.float32)
    normal_k = jax.random.normal(jax.random.fold_in(key, 102), (TOKENS, full_width), jnp.float32)
    return (normal_q, normal_k)


def draw_queries(key, part):
    normal_q, normal_k = shared_rows(key)
    result = 2.0 * jnp.clip(normal_q, -6.0, 6.0)
    return result.astype(jnp.bfloat16)


def draw_key_rows(key, part):
    normal_q, normal_k = shared_rows(key)
    result = jnp.clip(normal_k, -6.0, 6.0)
    return result.astype(jnp.bfloat16)


def draw_noise_level(key, part):
    key = jax.random.fold_in(key, 3)
    order_key, level_key = jax.random.split(key)
    order = jax.random.permutation(order_key, SPANS).astype(jnp.int32)
    levels = jax.random.randint(level_key, (SPANS,), 0, LEVELS).astype(jnp.int32)
    levels = jnp.where(order == 0, 0, levels)
    levels = jnp.where(order == SPANS - 1, LEVELS - 1, levels)
    return levels.astype(jnp.int32)


def draw_block_mask(key, part):
    key = jax.random.fold_in(key, 4)
    density_key, entry_key = jax.random.split(key)
    density = jax.random.randint(density_key, (SPANS, 1), 0, 9)
    entries = jax.random.randint(entry_key, (SPANS, SPANS), 0, 8)
    row_index = jnp.arange(SPANS, dtype=jnp.int32)[:, None]
    col_index = jnp.arange(SPANS, dtype=jnp.int32)[None, :]
    chosen = (entries < density) | (col_index == row_index) | (col_index == row_index - 1)
    return chosen.astype(jnp.int32)


def steps_of(own_key, shape, pieces, smallest, top_value):
    gain = 1.0
    for position, parts in pieces:
        draws = jax.random.uniform(jax.random.fold_in(jax.random.fold_in(own_key, 6), position), (parts,), jnp.float32, smallest / len(pieces), top_value / len(pieces))
        gain = gain * jnp.repeat(jnp.exp(draws), shape[position] // parts).reshape((-1,) + (1,) * (len(shape) - 1 - position))
    return gain


def profile(number_of, total, limit, skew):
    weights = [(1 << 20) // math.isqrt(standing ** skew) + 1 for standing in range(2, number_of + 1)]
    rest, given = total - limit - (number_of - 1), [1] * (number_of - 1)
    while rest > 0:
        free = [i for i in range(number_of - 1) if given[i] < limit]
        mass, left = sum([weights[i] for i in free]), rest
        for i in free:
            addition = min(limit - given[i], max(1, left * weights[i] // mass), rest)
            given[i] = given[i] + addition
            rest = rest - addition
    return np.array([limit] + given)


def ragged(key, amount, total, most, skew):
    if amount == 2:
        one = jax.random.randint(key, (), max(1, total - most), min(most, total - 1) + 1)
        return jnp.stack([one, total - one])
    sizes = jnp.asarray(profile(amount, total, most, skew), jnp.int32)
    twos = (amount - 1) // 2
    donor, taker = sizes[1:1 + 2 * twos:2], sizes[2:2 + 2 * twos:2]
    margin = jnp.minimum(donor - 1, most - taker)
    shifted = jax.random.randint(jax.random.fold_in(key, 1), (twos,), 0, 1 << 20) % (margin + 1)
    sizes = sizes.at[1:1 + 2 * twos:2].set(donor - shifted).at[2:2 + 2 * twos:2].set(taker + shifted)
    return sizes[jax.random.permutation(jax.random.fold_in(key, 2), amount)]


def normal_values(rng, extent, scale, bound, shards=(), kind=jnp.bfloat16):
    values = scale * jax.random.normal(rng, extent, jnp.float32)
    if shards:
        values = values * steps_of(rng, extent, shards, -0.22, 0.18)
    return jnp.clip(values, -bound, bound).astype(kind)


def setup_inputs(seed: int = 0) -> dict:
    streams_of = jax.random.split(jax.random.key(seed), 9)
    queries = draw_queries(jax.random.fold_in(streams_of[8], 71), 0)
    key_rows = draw_key_rows(jax.random.fold_in(streams_of[8], 71), 0)
    value_rows = normal_values(streams_of[2], (TOKENS, HEADS * DH), 1.0, 6.0, ((0, 256),))
    out_cotangent = normal_values(streams_of[3], (TOKENS, HEADS * DH), 1.0, 6.0, ((0, 256),))
    gate_table = normal_values(streams_of[4], (LEVELS, HEADS * DH), 1.5, 6.0, (), jnp.float32)
    span_ids = jnp.searchsorted(jnp.cumsum(ragged(streams_of[5], SPANS, TOKENS, SPAN, 0)), jnp.arange(TOKENS), side="right").astype(jnp.int32)
    noise_level = draw_noise_level(jax.random.fold_in(streams_of[8], 71), 0)
    block_mask = draw_block_mask(jax.random.fold_in(streams_of[8], 71), 0)
    return {"queries": queries, "key_rows": key_rows, "value_rows": value_rows, "out_cotangent": out_cotangent, "gate_table": gate_table, "span_ids": span_ids, "noise_level": noise_level, "block_mask": block_mask}


def attend(q_block, k_block, v_block, g_block, visible, score_scale):
    count_q = q_block.shape[0]
    count_k = k_block.shape[0]
    head_count = q_block.shape[1] // DH
    q_heads = q_block.astype(jnp.float32).reshape(count_q, head_count, DH)
    k_heads = k_block.astype(jnp.float32).reshape(count_k, head_count, DH)
    v_heads = v_block.astype(jnp.float32).reshape(count_k, head_count, DH)
    g_heads = g_block.astype(jnp.float32).reshape(count_q, head_count, DH)
    scores = jnp.einsum('qhd,khd->hqk', q_heads, k_heads) * score_scale
    scores = jnp.where(visible[None], scores, -jnp.inf)
    row_max = lax.optimization_barrier(jnp.max(scores, axis=2, keepdims=True))
    log_total = row_max + jnp.log(lax.optimization_barrier(jnp.sum(jnp.exp(scores - row_max), axis=2, keepdims=True)))
    attention = jnp.exp(scores - log_total)
    attention_low = attention.astype(jnp.bfloat16)
    attention_back = lax.optimization_barrier(attention_low).astype(jnp.float32)
    attended = jnp.einsum('hqk,khd->qhd', attention_back, v_heads).astype(jnp.bfloat16)
    attended_back = lax.optimization_barrier(attended).astype(jnp.float32)
    row_dot = jnp.einsum('qhd,qhd->hq', g_heads, attended_back)[:, :, None]
    prob_grad = jnp.einsum('qhd,khd->hqk', g_heads, v_heads)
    score_grad = (attention * (prob_grad - row_dot)).astype(jnp.bfloat16)
    score_back = lax.optimization_barrier(score_grad).astype(jnp.float32)
    query_grad = (jnp.einsum('hqk,khd->qhd', score_back, k_heads) * score_scale).astype(jnp.bfloat16)
    key_grad = jnp.einsum('hqk,qhd->khd', score_back, q_heads) * score_scale
    value_grad = jnp.einsum('hqk,qhd->khd', attention_back, g_heads)
    return (attended.reshape(count_q, -1), query_grad.reshape(count_q, -1), key_grad.reshape(count_k, -1), value_grad.reshape(count_k, -1))

def reference(queries, key_rows, value_rows, out_cotangent, gate_table, span_ids, noise_level, block_mask):
    full_width = HEADS * DH
    score_scale = 1.0 / math.sqrt(DH)
    q_size = min(512, WINDOW)
    k_size = WINDOW + q_size + SPAN
    token_level = jnp.take(noise_level, span_ids).astype(jnp.int32)
    level_onehot = (token_level[:, None] == jnp.arange(LEVELS, dtype=jnp.int32)[None, :]).astype(jnp.float32)
    gate_rows = jnp.dot(level_onehot, gate_table, precision=lax.Precision.HIGHEST)
    grad_attended = (gate_rows * out_cotangent.astype(jnp.float32)).astype(jnp.bfloat16)
    padding = ((WINDOW, SPAN), (0, 0))
    key_padded = jnp.pad(key_rows, padding)
    value_padded = jnp.pad(value_rows, padding)
    key_pos = jnp.arange(TOKENS + WINDOW + SPAN, dtype=jnp.int32) - WINDOW
    key_span = jnp.take(span_ids, jnp.clip(key_pos, 0, TOKENS - 1)).astype(jnp.int32)
    key_valid = (key_pos >= 0) & (key_pos < TOKENS)
    query_pos = jnp.arange(TOKENS, dtype=jnp.int32)

    def one_block(partials, offset):
        key_acc, value_acc = partials
        q_block = lax.dynamic_slice_in_dim(queries, offset, q_size, 0)
        g_block = lax.dynamic_slice_in_dim(grad_attended, offset, q_size, 0)
        k_block = lax.dynamic_slice_in_dim(key_padded, offset, k_size, 0)
        v_block = lax.dynamic_slice_in_dim(value_padded, offset, k_size, 0)
        span_q = lax.dynamic_slice_in_dim(span_ids, offset, q_size, 0)
        pos_q = lax.dynamic_slice_in_dim(query_pos, offset, q_size, 0)
        span_k = lax.dynamic_slice_in_dim(key_span, offset, k_size, 0)
        pos_k = lax.dynamic_slice_in_dim(key_pos, offset, k_size, 0)
        valid_k = lax.dynamic_slice_in_dim(key_valid, offset, k_size, 0)
        allowed = jnp.take(jnp.take(block_mask, span_q, axis=0), span_k, axis=1) == 1
        visible = allowed & (span_k[None, :] <= span_q[:, None]) & (pos_q[:, None] - pos_k[None, :] < WINDOW) & valid_k[None, :]
        attended, query_grad, key_grad, value_grad = attend(q_block, k_block, v_block, g_block, visible, score_scale)
        key_part = lax.dynamic_slice_in_dim(key_acc, offset, k_size, 0) + key_grad
        value_part = lax.dynamic_slice_in_dim(value_acc, offset, k_size, 0) + value_grad
        key_acc = lax.dynamic_update_slice_in_dim(key_acc, key_part, offset, 0)
        value_acc = lax.dynamic_update_slice_in_dim(value_acc, value_part, offset, 0)
        return ((key_acc, value_acc), (attended, query_grad))
    offsets = jnp.arange(0, TOKENS, q_size, dtype=jnp.int32)
    zero_rows = jnp.zeros((TOKENS + WINDOW + SPAN, full_width), jnp.float32)
    (key_acc, value_acc), (attended, query_grad) = lax.scan(one_block, (zero_rows, zero_rows), offsets)
    attended = attended.reshape(TOKENS, full_width)
    query_grad = query_grad.reshape(TOKENS, full_width)
    mixed_out = (gate_rows * attended.astype(jnp.float32)).astype(jnp.bfloat16)
    key_grad = key_acc[WINDOW:WINDOW + TOKENS].astype(jnp.bfloat16)
    value_grad = value_acc[WINDOW:WINDOW + TOKENS].astype(jnp.bfloat16)
    products = out_cotangent.astype(jnp.float32) * attended.astype(jnp.float32)
    gate_grad = jnp.dot(level_onehot.T, products, precision=lax.Precision.HIGHEST)
    return (mixed_out, query_grad, key_grad, value_grad, gate_grad)
```

```python
import functools
import math

import jax
import jax.numpy as jnp
from jax import lax
from jax.experimental import pallas as pl
from jax.experimental.pallas import tpu as pltpu
from jax.sharding import PartitionSpec as P

DH = 128
SPAN = 256
WINDOW = 1024
TILE = 256
SLAB = WINDOW + TILE + SPAN
BUF = 2 * WINDOW + SPAN
SCALE = 1.0 / math.sqrt(DH)
LOG2E = 1.0 / math.log(2.0)
HIDDEN = -1e30
F32 = jnp.float32
BF16 = jnp.bfloat16


def mm(a, b, contract=((1,), (0,))):
    return lax.dot_general(a, b, (contract, ((), ())), preferred_element_type=F32)


def prepare(span_ref, noise_ref, mask_ref, tab_ref, spans_k, bias, gate, level_t):
    spans = mask_ref.shape[0]
    levels = tab_ref.shape[1]
    row = lax.broadcasted_iota(jnp.int32, (spans, BUF), 0)
    onehot_t = (span_ref[...] == row).astype(F32)
    spans_k[...] = onehot_t.T.astype(BF16)
    own = onehot_t[:, WINDOW : 2 * WINDOW].astype(BF16)
    qs = lax.broadcasted_iota(jnp.int32, (spans, spans), 0)
    ks = lax.broadcasted_iota(jnp.int32, (spans, spans), 1)
    allowed = jnp.where(ks <= qs, mask_ref[...], 0).astype(F32).T.astype(BF16)
    mask_t = mm(allowed, own).astype(BF16)
    for t in range(WINDOW // TILE):
        seen = mm(spans_k[t * TILE : t * TILE + SLAB, :], mask_t[:, t * TILE : (t + 1) * TILE])
        bias[t] = jnp.where(seen > 0.5, 0.0, HIDDEN)
        k_pos = lax.broadcasted_iota(jnp.int32, (TILE, TILE), 0)
        q_pos = lax.broadcasted_iota(jnp.int32, (TILE, TILE), 1)
        bias[t, 0:TILE, :] = jnp.where(k_pos > q_pos, bias[t, 0:TILE, :], HIDDEN)
    lev = lax.broadcasted_iota(jnp.int32, (levels, spans), 0)
    span_level = (noise_ref[...] == lev).astype(BF16)
    level_t[...] = mm(span_level, own).astype(BF16)
    level = mm(spans_k[WINDOW : 2 * WINDOW, :], span_level, ((1,), (1,))).astype(BF16)
    for h in range(tab_ref.shape[0]):
        table = tab_ref[h]
        high = table.astype(BF16)
        low = (table - high.astype(F32)).astype(BF16)
        gate[h] = mm(level, high) + mm(level, low)


def attend_head(h, kv, qg, bias, gate, level_t, acc, res, gate_part):
    acc[...] = jnp.zeros_like(acc)

    def tile(t, level_sum):
        q_at = pl.ds(pl.multiple_of(t * TILE, TILE), TILE)
        k_at = pl.ds(pl.multiple_of(t * TILE, TILE), SLAB)
        k = kv[h, 0, k_at, :]
        v = kv[h, 1, k_at, :]
        q = qg[h, 0, q_at, :]
        cot = qg[h, 1, q_at, :].astype(F32)
        gate_rows = gate[h, q_at, :]
        g = (gate_rows * cot).astype(BF16)
        g_t = g.astype(F32).T
        z = mm(k, q, ((1,), (1,))) * (SCALE * LOG2E) + bias[t]
        top = jnp.max(z, axis=0, keepdims=True)
        e = jnp.exp2(z - top)
        inv = 1.0 / jnp.sum(e, axis=0, keepdims=True)
        e_low = e.astype(BF16)
        att_t = (mm(v, e_low, ((0,), (0,))) * inv).astype(BF16).astype(F32)
        dot = jnp.sum(g_t * att_t, axis=0, keepdims=True) * inv
        gs_t = (g_t * inv).astype(BF16)
        att = att_t.T
        d_prob = mm(v, gs_t)
        ds = (e * (d_prob - dot)).astype(BF16)
        acc[1, k_at, :] += mm(e_low, gs_t, ((1,), (1,)))
        acc[0, k_at, :] += mm(ds, q)
        dq_t = mm(k, ds, ((0,), (0,))) * SCALE
        res[h, 0, q_at, :] = (gate_rows * att).astype(BF16)
        res[h, 1, q_at, :] = dq_t.T.astype(BF16)
        prod = cot * att
        high = prod.astype(BF16)
        low = (prod - high.astype(F32)).astype(BF16)
        lev = level_t[:, q_at]
        return level_sum + mm(lev, high) + mm(lev, low)

    zero = jnp.zeros((level_t.shape[0], DH), F32)
    gate_part[h] = lax.fori_loop(0, WINDOW // TILE, tile, zero)


def kernel(span_ref, noise_ref, mask_ref, tab_ref, kv, qg, res, own, behind, ahead, gate_part,
           spans_k, bias, gate, level_t, acc):
    prepare(span_ref, noise_ref, mask_ref, tab_ref, spans_k, bias, gate, level_t)
    for h in range(kv.shape[0]):
        attend_head(h, kv, qg, bias, gate, level_t, acc, res, gate_part)
        for i, s in ((0, SCALE), (1, 1.0)):
            behind[h, i] = (acc[i, 0:WINDOW, :] * s).astype(BF16)
            own[h, i] = acc[i, WINDOW : 2 * WINDOW, :] * s
            ahead[h, i] = (acc[i, 2 * WINDOW :, :] * s).astype(BF16)


def attention(spans, noise, mask, tab, kv, qg):
    heads = kv.shape[0]
    vmem = pl.BlockSpec(memory_space=pltpu.VMEM)
    span_total = mask.shape[0]
    levels = tab.shape[1]
    return pl.pallas_call(
        kernel,
        out_shape=[
            jax.ShapeDtypeStruct((heads, 2, WINDOW, DH), BF16),
            jax.ShapeDtypeStruct((heads, 2, WINDOW, DH), F32),
            jax.ShapeDtypeStruct((heads, 2, WINDOW, DH), BF16),
            jax.ShapeDtypeStruct((heads, 2, SPAN, DH), BF16),
            jax.ShapeDtypeStruct((heads, levels, DH), F32),
        ],
        in_specs=[vmem] * 6,
        out_specs=[vmem] * 5,
        scratch_shapes=[
            pltpu.VMEM((BUF, span_total), BF16),
            pltpu.VMEM((WINDOW // TILE, SLAB, TILE), F32),
            pltpu.VMEM((heads, WINDOW, DH), F32),
            pltpu.VMEM((levels, WINDOW), BF16),
            pltpu.VMEM((2, BUF, DH), F32),
        ],
        compiler_params=pltpu.CompilerParams(vmem_limit_bytes=56 * 1024 * 1024),
    )(spans, noise, mask, tab, kv, qg)


def shifted(x, by):
    n = lax.axis_size("ctx")
    return lax.ppermute(x, "ctx", [(i, (i + by) % n) for i in range(n)])


def per_device(queries, key_rows, value_rows, out_cotangent, gate_table, span_ids, noise_level, block_mask):
    groups = lax.axis_size("head")
    rows, width = queries.shape
    heads = width // groups // DH
    ctx = lax.axis_index("ctx")
    head = lax.axis_index("head")
    padded = jnp.pad(span_ids, (WINDOW, SPAN), constant_values=-1)
    spans = lax.dynamic_slice_in_dim(padded, ctx * WINDOW, BUF, 0)[None, :]
    tab = lax.dynamic_slice_in_dim(gate_table, head * heads * DH, heads * DH, 1)
    tab = tab.reshape(-1, heads, DH).transpose(1, 0, 2)

    def to_heads(*arrays):
        x = jnp.stack(arrays).reshape(len(arrays), rows, groups, heads, DH).transpose(2, 3, 0, 1, 4)
        x = lax.all_to_all(x, "head", 0, 0, tiled=True)
        return x.transpose(1, 2, 0, 3, 4).reshape(heads, len(arrays), WINDOW, DH)

    def to_tokens(x):
        x = x.reshape(heads, 2, groups, rows, DH).transpose(2, 0, 1, 3, 4)
        x = lax.all_to_all(x, "head", 0, 0, tiled=True)
        x = x.transpose(2, 3, 0, 1, 4).reshape(2, rows, width)
        return x[0], x[1]

    kv_own = to_heads(key_rows, value_rows)
    qg = to_heads(queries, out_cotangent)
    kv = jnp.concatenate([shifted(kv_own, 1), kv_own, shifted(kv_own[:, :, :SPAN], -1)], axis=2)
    res, own, behind, ahead, gate_part = attention(
        spans, noise_level[None, :], block_mask, tab, kv, qg
    )
    own = own + shifted(behind, -1).astype(F32)
    own = own.at[:, :, :SPAN].add(shifted(ahead, 1).astype(F32))
    gate_sum = lax.psum(gate_part, "ctx")
    gate_grad = lax.all_gather(gate_sum, "head", axis=0, tiled=True)
    gate_grad = gate_grad.transpose(1, 0, 2).reshape(-1, width)
    mixed_out, query_grad = to_tokens(res)
    key_grad, value_grad = to_tokens(own.astype(BF16))
    return mixed_out, query_grad, key_grad, value_grad, gate_grad


def solution(mesh):
    split = P(("ctx", "head"), None)
    return jax.shard_map(
        per_device,
        mesh=mesh,
        in_specs=(split, split, split, split, P(), P(), P(), P()),
        out_specs=(split, split, split, split, P()),
        check_vma=False,
    )
```

```python
import functools
import math

import jax
import jax.numpy as jnp
from jax import lax
from jax.experimental import pallas as pl
from jax.experimental.pallas import tpu as pltpu
from jax.sharding import PartitionSpec as P

DH = 128
SPAN = 256
WINDOW = 1024
TILE = 256
BLOCK = 128
SLAB = WINDOW + TILE + SPAN
QA = 2 * WINDOW
QB = WINDOW
PLANE = 4 * WINDOW
SCALE = 1.0 / math.sqrt(DH)
LOG2E = 1.0 / math.log(2.0)
HIDDEN = -1e30
F32 = jnp.float32
BF16 = jnp.bfloat16
MESH = pl.DeviceIdType.MESH


def mm(a, b, contract=((1,), (0,))):
    return lax.dot_general(a, b, (contract, ((), ())), preferred_element_type=F32)


def place(z, x, y, core):
    return (z * 4 + lax.rem(x, 2) * 2 + core, lax.div(x, 2) * 4 + y)


def where_am_i():
    ctx = lax.axis_index("ctx")
    head = lax.axis_index("head")
    z = lax.div(ctx, 4)
    x = lax.div(head, 4) * 2 + lax.rem(lax.div(ctx, 2), 2)
    return z, x, lax.rem(head, 4), lax.rem(ctx, 2)


def whole_head(x, y):
    return x * 4 + y


def shared_head(x, y):
    return 16 + lax.div(x, 2) * 4 + y


def prepare(span_ref, noise_ref, mask_ref, tab_ref, spans_k, bias, gate, level_t):
    spans = mask_ref.shape[0]
    levels = tab_ref.shape[0]
    queries = bias.shape[0] * TILE
    rows = queries + WINDOW + SPAN
    row = lax.broadcasted_iota(jnp.int32, (spans, rows), 0)
    onehot_t = (span_ref[...] == row).astype(F32)
    spans_k[0:rows, :] = onehot_t.T.astype(BF16)
    own = onehot_t[:, WINDOW : WINDOW + queries].astype(BF16)
    qs = lax.broadcasted_iota(jnp.int32, (spans, spans), 0)
    ks = lax.broadcasted_iota(jnp.int32, (spans, spans), 1)
    allowed = jnp.where(ks <= qs, mask_ref[...], 0).astype(F32).T.astype(BF16)
    mask_t = mm(allowed, own).astype(BF16)
    k_pos = lax.broadcasted_iota(jnp.int32, (TILE, TILE), 0)
    q_pos = lax.broadcasted_iota(jnp.int32, (TILE, TILE), 1)
    for t in range(bias.shape[0]):
        seen = mm(spans_k[t * TILE : t * TILE + SLAB, :], mask_t[:, t * TILE : (t + 1) * TILE])
        shown = jnp.where(seen > 0.5, 0.0, HIDDEN)
        bias[t, TILE:, :] = shown[TILE:, :]
        bias[t, 0:TILE, :] = jnp.where(k_pos > q_pos, shown[0:TILE, :], HIDDEN)
    lev = lax.broadcasted_iota(jnp.int32, (levels, spans), 0)
    span_level = (noise_ref[...] == lev).astype(BF16)
    level_t[...] = mm(span_level, own).astype(BF16)
    level = mm(spans_k[WINDOW : WINDOW + queries, :], span_level, ((1,), (1,))).astype(BF16)
    table = tab_ref[...]
    high = table.astype(BF16)
    low = (table - high.astype(F32)).astype(BF16)
    gate[...] = mm(level, high) + mm(level, low)


def attend_tile(t, kv, qg, bias, gate, level_t, acc, res, level_sum):
    q_at = pl.ds(pl.multiple_of(t * TILE, TILE), TILE)
    k_at = pl.ds(pl.multiple_of(t * TILE, TILE), SLAB)
    k = kv[0, k_at, :]
    v = kv[1, k_at, :]
    q = qg[0, q_at, :]
    cot = qg[1, q_at, :].astype(F32)
    gate_rows = gate[q_at, :]
    g_t = (gate_rows * cot).astype(BF16).astype(F32).T
    z = mm(k, q, ((1,), (1,))) * (SCALE * LOG2E) + bias[t]
    top = jnp.max(z, axis=0, keepdims=True)
    e = jnp.exp2(z - top)
    inv = 1.0 / jnp.sum(e, axis=0, keepdims=True)
    e_low = e.astype(BF16)
    att_t = (mm(v, e_low, ((0,), (0,))) * inv).astype(BF16).astype(F32)
    dot = jnp.sum(g_t * att_t, axis=0, keepdims=True) * inv
    gs_t = (g_t * inv).astype(BF16)
    att = att_t.T
    d_prob = mm(v, gs_t)
    ds = (e * (d_prob - dot)).astype(BF16)
    acc[1, k_at, :] += mm(e_low, gs_t, ((1,), (1,)))
    acc[0, k_at, :] += mm(ds, q)
    dq_t = mm(k, ds, ((0,), (0,))) * SCALE
    res[0, q_at, :] = (gate_rows * att).astype(BF16)
    res[1, q_at, :] = dq_t.T.astype(BF16)
    prod = cot * att
    high = prod.astype(BF16)
    low = (prod - high.astype(F32)).astype(BF16)
    lev = level_t[:, q_at]
    level_sum[...] += mm(lev, high) + mm(lev, low)


def kernel(
    nz, span_a, span_b, noise_ref, mask_ref, tab_a, tab_b, q_ref, k_ref, v_ref, c_ref,
    out_mq, out_kv, out_gate,
    st_kv, st_qg, kv_a, kv_b, qg_a, qg_b, spans_k, bias_a, bias_b, gate_a, gate_b, lev_a, lev_b,
    acc_a, acc_b, res_a, res_b, dkv_a, dkv_b, sb_a, sb_b, sa_a, sa_b, rb_a, rb_b, ra_a, ra_b,
    gate_part, gate_pair, gate_all, pieces, sums, full, full_low, gate_buf,
    load_sem, in_send, in_recv, halo_send, halo_recv, part_send, part_recv, out_send, out_recv,
    gate_send, gate_recv,
):
    z, x, y, core = where_am_i()
    x_lo = lax.rem(x, 2)
    own_block = lax.div(x, 2) * 4 + y
    stays = core == x_lo
    pair_x = x + 1 - 2 * x_lo
    group = 2 * nz
    member = z * 2 + core
    piece = sums.shape[1]

    def remote(src, dst, send, recv, to):
        return pltpu.make_async_remote_copy(
            src_ref=src, dst_ref=dst, send_sem=send, recv_sem=recv, device_id=to, device_id_type=MESH
        )

    def took(ref, sem):
        pltpu.make_async_copy(ref, ref, sem).wait()

    def cols(head):
        return pl.ds(pl.multiple_of(head * DH, DH), DH)

    def rows(start, size):
        return pl.ds(pl.multiple_of(start, BLOCK), size)

    loads = [
        pltpu.make_async_copy(src, st.at[i], load_sem.at[n])
        for n, (src, st, i) in enumerate(
            ((k_ref, st_kv, 0), (v_ref, st_kv, 1), (q_ref, st_qg, 0), (c_ref, st_qg, 1))
        )
    ]
    for load in loads:
        load.start()

    barrier = pltpu.get_barrier_semaphore()
    spot = x * 8 + y * 2 + core

    def greet_plane(j, carry):
        other = lax.rem(spot + j, 32)
        to = place(z, lax.div(other, 8), lax.rem(lax.div(other, 2), 4), lax.rem(other, 2))
        pl.semaphore_signal(barrier, inc=1, device_id=to, device_id_type=MESH)
        return carry

    lax.fori_loop(1, 32, greet_plane, 0)

    def greet_column(j, carry):
        for c in range(2):
            to = place(lax.rem(z + j, nz), x, y, c)
            pl.semaphore_signal(barrier, inc=1, device_id=to, device_id_type=MESH)
        return carry

    lax.fori_loop(1, nz, greet_column, 0)
    for step in (1, nz - 1):
        to = place(lax.rem(z + step, nz), pair_x, y, 1 - core)
        pl.semaphore_signal(barrier, inc=1, device_id=to, device_id_type=MESH)
    pl.semaphore_wait(barrier, 31 + 2 * (nz - 1) + 2)

    def send_shared(st, dst, s):
        start = own_block * BLOCK
        at = dst.at[:, rows(WINDOW + start if dst is kv_b else start, BLOCK), :]
        for j in range(8):
            tx = lax.rem(x + 2 * (j % 2), 4)
            ty = lax.rem(y + j // 2, 4)
            src = st.at[:, :, cols(shared_head(tx, ty))]
            if j == 0:
                pltpu.make_async_copy(src, at, in_recv.at[s]).start()
            else:
                remote(src, at, in_send.at[s], in_recv.at[s], place(z, tx, ty, core)).start()

    def send_whole(st, dst, s):
        start = core * WINDOW + own_block * BLOCK
        at = dst.at[:, rows(WINDOW + start if dst is kv_a else start, BLOCK), :]
        for j in range(16):
            tx = lax.rem(x + j % 4, 4)
            ty = lax.rem(y + j // 4, 4)
            src = st.at[:, :, cols(whole_head(tx, ty))]
            go = remote(src, at, in_send.at[s], in_recv.at[s], place(z, tx, ty, x_lo))
            if j == 0:
                @pl.when(stays)
                def _():
                    pltpu.make_async_copy(src, at, in_recv.at[s]).start()

                @pl.when(jnp.logical_not(stays))
                def _():
                    go.start()
            else:
                go.start()

    loads[0].wait()
    loads[1].wait()
    send_shared(st_kv, kv_b, 0)
    loads[2].wait()
    loads[3].wait()
    send_shared(st_qg, qg_b, 1)
    send_whole(st_kv, kv_a, 2)

    prepare(span_b, noise_ref, mask_ref, tab_b, spans_k, bias_b, gate_b, lev_b)
    acc_b[...] = jnp.zeros_like(acc_b)
    gate_part[...] = jnp.zeros_like(gate_part)

    next_a = place(lax.rem(z + core, nz), x, y, 1 - core)
    prev_a = place(lax.rem(z + nz - 1 + core, nz), x, y, 1 - core)
    next_x = jnp.where(core == 0, x, pair_x)
    prev_x = jnp.where(core == 0, pair_x, x)
    next_b = place(lax.rem(z + core * x_lo, nz), next_x, y, 1 - core)
    prev_b = place(lax.rem(z + nz - (1 - core) * (1 - x_lo), nz), prev_x, y, 1 - core)

    def halo(kv, queries, n, after, before):
        last = WINDOW + queries
        return (
            remote(
                kv.at[:, queries:last, :], kv.at[:, 0:WINDOW, :], halo_send.at[n], halo_recv.at[n], after
            ),
            remote(
                kv.at[:, WINDOW : WINDOW + SPAN, :],
                kv.at[:, last : last + SPAN, :],
                halo_send.at[n + 1],
                halo_recv.at[n + 1],
                before,
            ),
        )

    halo_b = halo(kv_b, QB, 0, next_b, prev_b)
    halo_a = halo(kv_a, QA, 2, next_a, prev_a)

    took(kv_b.at[:, WINDOW : WINDOW + QB, :], in_recv.at[0])
    for c in halo_b:
        c.start()
    send_whole(st_qg, qg_a, 3)
    prepare(span_a, noise_ref, mask_ref, tab_a, spans_k, bias_a, gate_a, lev_a)
    acc_a[...] = jnp.zeros_like(acc_a)
    took(qg_b, in_recv.at[1])
    for c in halo_b:
        c.wait()

    def give_shared(buf, out, i, s):
        src = buf.at[:, rows(i * BLOCK, BLOCK), :]
        dst = out.at[:, :, cols(shared_head(x, y))]
        mine = i == own_block

        @pl.when(mine)
        def _():
            pltpu.make_async_copy(src, dst, out_recv.at[s]).start()

        @pl.when(jnp.logical_not(mine))
        def _():
            to = place(z, lax.div(i, 4) * 2 + x_lo, lax.rem(i, 4), core)
            remote(src, dst, out_send.at[s], out_recv.at[s], to).start()

    def give_whole(buf, out, i, s):
        src = buf.at[:, rows(i * BLOCK, BLOCK), :]
        dst = out.at[:, :, cols(whole_head(x, y))]
        mine = jnp.logical_and(stays, i == core * 8 + own_block)

        @pl.when(mine)
        def _():
            pltpu.make_async_copy(src, dst, out_recv.at[s]).start()

        @pl.when(jnp.logical_not(mine))
        def _():
            b = lax.rem(i, 8)
            to = place(z, lax.div(b, 4) * 2 + core, lax.rem(b, 4), lax.div(i, 8))
            remote(src, dst, out_send.at[2 + s], out_recv.at[s], to).start()

    def tile_b(t, carry):
        attend_tile(t, kv_b, qg_b, bias_b, gate_b, lev_b, acc_b, res_b, gate_part.at[1])
        for j in range(TILE // BLOCK):
            give_shared(res_b, out_mq, t * (TILE // BLOCK) + j, 0)
        return carry

    lax.fori_loop(0, QB // TILE, tile_b, 0)

    def part(buf, recv, n, to):
        return remote(buf, recv, part_send.at[n], part_recv.at[n], to)

    behind_b = part(sb_b, rb_b, 0, prev_b)
    ahead_b = part(sa_b, ra_b, 1, next_b)
    behind_a = part(sb_a, rb_a, 2, prev_a)
    ahead_a = part(sa_a, ra_a, 3, next_a)
    pair_gate = remote(
        gate_part.at[1], gate_pair, gate_send.at[0], gate_recv.at[0], place(z, pair_x, y, core)
    )

    for i, s in ((0, SCALE), (1, 1.0)):
        sb_b[i] = (acc_b[i, 0:WINDOW, :] * s).astype(BF16)
        sa_b[i] = (acc_b[i, WINDOW + QB :, :] * s).astype(BF16)
    behind_b.start()
    ahead_b.start()
    pair_gate.start()

    took(kv_a.at[:, WINDOW : WINDOW + QA, :], in_recv.at[2])
    for c in halo_a:
        c.start()
    took(qg_a, in_recv.at[3])
    for c in halo_a:
        c.wait()

    def finish_b():
        behind_b.wait()
        ahead_b.wait()
        for i, s in ((0, SCALE), (1, 1.0)):
            total = acc_b[i, WINDOW : WINDOW + QB, :] * s + rb_b[i].astype(F32)
            dkv_b[i] = total.astype(BF16)
            first = total[0:SPAN, :] + ra_b[i].astype(F32)
            dkv_b[i, 0:SPAN, :] = first.astype(BF16)

        def give(i, carry):
            give_shared(dkv_b, out_kv, i, 1)
            return carry

        lax.fori_loop(0, QB // BLOCK, give, 0)

    def tile_a(t, carry):
        attend_tile(t, kv_a, qg_a, bias_a, gate_a, lev_a, acc_a, res_a, gate_part.at[0])
        for j in range(TILE // BLOCK):
            give_whole(res_a, out_mq, t * (TILE // BLOCK) + j, 0)

        @pl.when(t == 1)
        def _():
            finish_b()

        @pl.when(t == 3)
        def _():
            for i, s in ((0, SCALE), (1, 1.0)):
                sb_a[i] = (acc_a[i, 0:WINDOW, :] * s).astype(BF16)
            behind_a.start()

        @pl.when(t >= 5)
        def _():
            own = pl.ds(pl.multiple_of((t - 4) * TILE, TILE), TILE)
            held = pl.ds(pl.multiple_of(t * TILE, TILE), TILE)
            dkv_a[0, own, :] = (acc_a[0, held, :] * SCALE).astype(BF16)
            dkv_a[1, own, :] = acc_a[1, held, :].astype(BF16)
            for j in range(TILE // BLOCK):
                give_whole(dkv_a, out_kv, (t - 4) * (TILE // BLOCK) + j, 1)

        return carry

    lax.fori_loop(0, QA // TILE, tile_a, 0)

    for i, s in ((0, SCALE), (1, 1.0)):
        sa_a[i] = (acc_a[i, WINDOW + QA :, :] * s).astype(BF16)
    ahead_a.start()

    pair_gate.wait()
    gate_all[0] = gate_part[0]
    gate_all[1] = gate_part[1] + gate_pair[...]
    at_mine = pl.ds(pl.multiple_of(member * piece, 8), piece)

    def to_member(j, carry):
        other = lax.rem(member + j, group)
        src = gate_all.at[:, pl.ds(pl.multiple_of(other * piece, 8), piece), :]
        to = place(lax.div(other, 2), x, y, lax.rem(other, 2))
        remote(src, pieces.at[member], gate_send.at[1], gate_recv.at[1], to).start()
        return carry

    lax.fori_loop(1, group, to_member, 0)

    def give_rest(i, carry):
        give_whole(dkv_a, out_kv, i, 1)
        return carry

    behind_a.wait()
    for i, s in ((0, SCALE), (1, 1.0)):
        total = acc_a[i, 2 * WINDOW : 2 * WINDOW + WINDOW, :] * s + rb_a[i].astype(F32)
        dkv_a[i, WINDOW:, :] = total.astype(BF16)
    lax.fori_loop(WINDOW // BLOCK, QA // BLOCK, give_rest, 0)

    took(pieces.at[0 : group - 1], gate_recv.at[1])
    total = gate_all[:, at_mine, :]
    for j in range(1, group):
        total = total + pieces[lax.rem(member + j, group)]
    sums[...] = total
    full[at_mine, :] = sums[core]

    def back_to_member(j, carry):
        other = lax.rem(member + j, group)
        c = lax.rem(other, 2)
        to = place(lax.div(other, 2), x, y, c)
        remote(sums.at[c], full.at[at_mine, :], gate_send.at[2], gate_recv.at[2], to).start()
        return carry

    lax.fori_loop(1, group, back_to_member, 0)

    ahead_a.wait()
    for i, s in ((0, SCALE), (1, 1.0)):
        first = acc_a[i, WINDOW : WINDOW + SPAN, :] * s + ra_a[i].astype(F32)
        dkv_a[i, 0:SPAN, :] = first.astype(BF16)
    lax.fori_loop(0, SPAN // BLOCK, give_rest, 0)

    took(full.at[0 : (group - 1) * piece, :], gate_recv.at[2])
    full_low[...] = full[...].astype(BF16)
    half = DH // 2
    at_half = pl.ds(pl.multiple_of(x_lo * half, half), half)
    other_core = place(z, x, y, 1 - core)
    split = whole_head(4, 0) * DH

    @pl.when(core == 0)
    def _():
        for j in range(1, 16):
            to = place(z, lax.rem(x + j % 4, 4), lax.rem(y + j // 4, 4), core)
            dst = gate_buf.at[:, cols(whole_head(x, y))]
            remote(full_low, dst, gate_send.at[3], gate_recv.at[3], to).start()
        gate_buf[:, cols(whole_head(x, y))] = full_low[...]
        took(gate_buf.at[:, 0 : 15 * DH], gate_recv.at[3])
        mine = gate_buf.at[:, 0:split]
        remote(mine, mine, gate_send.at[4], gate_recv.at[4], other_core).start()
        took(gate_buf.at[:, split:], gate_recv.at[4])

    @pl.when(core == 1)
    def _():
        for j in range(1, 16):
            to = place(z, lax.rem(x + j % 4, 4), lax.rem(y + j // 4, 4), core)
            dst = gate_buf.at[at_half, cols(shared_head(x, y))]
            remote(full_low.at[at_half, :], dst, gate_send.at[3], gate_recv.at[3], to).start()
        gate_buf[at_half, cols(shared_head(x, y))] = full_low[at_half, :]
        took(gate_buf.at[0:half, 0 : 15 * DH], gate_recv.at[3])
        mine = gate_buf.at[:, split:]
        remote(mine, mine, gate_send.at[4], gate_recv.at[4], other_core).start()
        took(gate_buf.at[:, 0:split], gate_recv.at[4])

    out_gate[...] = gate_buf[...].astype(F32)

    @pl.when(core == 0)
    def _():
        took(gate_buf.at[:, 0 : 15 * DH], gate_send.at[3])
        took(gate_buf.at[:, 0:split], gate_send.at[4])

    @pl.when(core == 1)
    def _():
        took(gate_buf.at[0:half, 0 : 15 * DH], gate_send.at[3])
        took(gate_buf.at[:, split:], gate_send.at[4])

    took(pieces.at[0 : group - 1], gate_send.at[1])
    took(full.at[0 : (group - 1) * piece, :], gate_send.at[2])
    for s in range(2):
        took(st_kv.at[:, :, 0 : 7 * DH], in_send.at[s])
        took(st_kv.at[:, :, 0 : 7 * DH], out_send.at[s])

    @pl.when(stays)
    def _():
        for s in range(2):
            took(st_kv.at[:, :, 0 : 15 * DH], in_send.at[2 + s])
            took(st_kv.at[:, :, 0 : 15 * DH], out_send.at[2 + s])

    @pl.when(jnp.logical_not(stays))
    def _():
        for s in range(2):
            took(st_kv.at[:, :, 0 : 16 * DH], in_send.at[2 + s])
            took(st_kv.at[:, :, 0 : 16 * DH], out_send.at[2 + s])

    took(out_mq, out_recv.at[0])
    took(out_kv, out_recv.at[1])


def fused(nz, spans_a, spans_b, noise, mask, tab_a, tab_b, q, k, v, c):
    vmem = pl.BlockSpec(memory_space=pltpu.VMEM)
    hbm = pl.BlockSpec(memory_space=pl.ANY)
    block, width = q.shape
    spans = mask.shape[0]
    levels = tab_a.shape[0]
    piece = levels // (2 * nz)

    def low(*shape):
        return pltpu.VMEM(shape, BF16)

    def wide(*shape):
        return pltpu.VMEM(shape, F32)

    def sems(n):
        return pltpu.SemaphoreType.DMA((n,))

    rows_a, rows_b = QA + WINDOW + SPAN, QB + WINDOW + SPAN
    return pl.pallas_call(
        functools.partial(kernel, nz),
        out_shape=[
            jax.ShapeDtypeStruct((2, block, width), BF16),
            jax.ShapeDtypeStruct((2, block, width), BF16),
            jax.ShapeDtypeStruct((levels, width), F32),
        ],
        in_specs=[vmem] * 6 + [hbm] * 4,
        out_specs=[hbm, hbm, vmem],
        scratch_shapes=[
            low(2, block, width), low(2, block, width),
            low(2, rows_a, DH), low(2, rows_b, DH), low(2, QA, DH), low(2, QB, DH),
            low(rows_a, spans),
            wide(QA // TILE, SLAB, TILE), wide(QB // TILE, SLAB, TILE),
            wide(QA, DH), wide(QB, DH), low(levels, QA), low(levels, QB),
            wide(2, rows_a, DH), wide(2, rows_b, DH),
            low(2, QA, DH), low(2, QB, DH), low(2, QA, DH), low(2, QB, DH),
            low(2, WINDOW, DH), low(2, WINDOW, DH), low(2, SPAN, DH), low(2, SPAN, DH),
            low(2, WINDOW, DH), low(2, WINDOW, DH), low(2, SPAN, DH), low(2, SPAN, DH),
            wide(2, levels, DH), wide(levels, DH), wide(2, levels, DH),
            wide(2 * nz, 2, piece, DH), wide(2, piece, DH), wide(levels, DH),
            low(levels, DH), low(levels, width),
            sems(4), sems(4), sems(4), sems(4), sems(4), sems(4), sems(4), sems(4), sems(2),
            sems(5), sems(5),
        ],
        compiler_params=pltpu.CompilerParams(
            collective_id=0, has_side_effects=True, vmem_limit_bytes=60 * 1024 * 1024
        ),
    )(spans_a, spans_b, noise, mask, tab_a, tab_b, q, k, v, c)


def per_device(queries, key_rows, value_rows, out_cotangent, gate_table, span_ids, noise_level, block_mask):
    nz = lax.axis_size("ctx") // 4
    z, x, y, core = where_am_i()
    padded = jnp.pad(span_ids, (WINDOW, SPAN), constant_values=-1)
    start_a = z * PLANE + core * QA
    start_b = z * PLANE + (lax.rem(x, 2) * 2 + core) * QB
    spans_a = lax.dynamic_slice_in_dim(padded, start_a, QA + WINDOW + SPAN, 0)[None, :]
    spans_b = lax.dynamic_slice_in_dim(padded, start_b, QB + WINDOW + SPAN, 0)[None, :]
    tab_a = lax.dynamic_slice_in_dim(gate_table, whole_head(x, y) * DH, DH, 1)
    tab_b = lax.dynamic_slice_in_dim(gate_table, shared_head(x, y) * DH, DH, 1)
    mq, kv, gate_grad = fused(
        nz, spans_a, spans_b, noise_level[None, :], block_mask, tab_a, tab_b,
        queries, key_rows, value_rows, out_cotangent,
    )
    return mq[0], mq[1], kv[0], kv[1], gate_grad


def solution(mesh):
    split = P(("ctx", "head"), None)
    return jax.shard_map(
        per_device,
        mesh=mesh,
        in_specs=(split, split, split, split, P(), P(), P(), P()),
        out_specs=(split, split, split, split, P()),
        check_vma=False,
    )
```

```python
import functools
import math

import jax
import jax.numpy as jnp
from jax import lax
from jax.experimental import pallas as pl
from jax.experimental.pallas import tpu as pltpu
from jax.sharding import PartitionSpec as P

DH = 128
SPAN = 256
WINDOW = 1024
TILE = 256
BLOCK = 128
SLAB = WINDOW + TILE + SPAN
QA = 2 * WINDOW
QB = WINDOW
PLANE = 4 * WINDOW
SCALE = 1.0 / math.sqrt(DH)
LOG2E = 1.0 / math.log(2.0)
HIDDEN = -1e30
F32 = jnp.float32
BF16 = jnp.bfloat16
MESH = pl.DeviceIdType.MESH


def mm(a, b, contract=((1,), (0,))):
    return lax.dot_general(a, b, (contract, ((), ())), preferred_element_type=F32)


def place(z, x, y, core):
    return (z * 4 + lax.rem(x, 2) * 2 + core, lax.div(x, 2) * 4 + y)


def where_am_i():
    ctx = lax.axis_index("ctx")
    head = lax.axis_index("head")
    z = lax.div(ctx, 4)
    x = lax.div(head, 4) * 2 + lax.rem(lax.div(ctx, 2), 2)
    return z, x, lax.rem(head, 4), lax.rem(ctx, 2)


def whole_head(x, y):
    return y * 4 + x


def shared_head(x, y):
    return 16 + y * 2 + lax.div(x, 2)


def prepare(start, span_ref, noise_ref, mask_ref, tab_ref, spans_t, spans_k, bias, gate, level_t):
    spans = mask_ref.shape[0]
    levels = tab_ref.shape[0]
    queries = bias.shape[0] * TILE
    rows = queries + WINDOW + SPAN
    total = span_ref.shape[0]
    first = lax.div(start, BLOCK) - WINDOW // BLOCK
    row = lax.broadcasted_iota(jnp.int32, (spans, BLOCK), 0)

    def encode(i, carry):
        block = first + i
        inside = jnp.logical_and(block >= 0, block < total)
        ids = span_ref[pl.ds(lax.rem(block + total, total), 1), :]
        onehot = (jnp.where(inside, ids, -1) == row).astype(F32)
        at = pl.ds(pl.multiple_of(i * BLOCK, BLOCK), BLOCK)
        spans_t[:, at] = onehot.astype(BF16)
        spans_k[at, :] = onehot.T.astype(BF16)
        return carry

    lax.fori_loop(0, rows // BLOCK, encode, 0)
    own = spans_t[:, WINDOW : WINDOW + queries]
    qs = lax.broadcasted_iota(jnp.int32, (spans, spans), 0)
    ks = lax.broadcasted_iota(jnp.int32, (spans, spans), 1)
    allowed = jnp.where(ks <= qs, mask_ref[...], 0).astype(F32).T.astype(BF16)
    mask_t = mm(allowed, own).astype(BF16)
    k_pos = lax.broadcasted_iota(jnp.int32, (TILE, TILE), 0)
    q_pos = lax.broadcasted_iota(jnp.int32, (TILE, TILE), 1)
    for t in range(bias.shape[0]):
        seen = mm(spans_k[t * TILE : t * TILE + SLAB, :], mask_t[:, t * TILE : (t + 1) * TILE])
        shown = jnp.where(seen > 0.5, 0.0, HIDDEN)
        bias[t, TILE:, :] = shown[TILE:, :]
        bias[t, 0:TILE, :] = jnp.where(k_pos > q_pos, shown[0:TILE, :], HIDDEN)
    lev = lax.broadcasted_iota(jnp.int32, (levels, spans), 0)
    span_level = (noise_ref[...] == lev).astype(BF16)
    level_t[...] = mm(span_level, own).astype(BF16)
    level = mm(spans_k[WINDOW : WINDOW + queries, :], span_level, ((1,), (1,))).astype(BF16)
    table = tab_ref[...]
    high = table.astype(BF16)
    low = (table - high.astype(F32)).astype(BF16)
    gate[...] = mm(level, high) + mm(level, low)


FAR_FIRST = sorted(
    ((jx, jy) for jy in range(4) for jx in range(4)),
    key=lambda j: -(min(j[0], 4 - j[0]) + min(j[1], 4 - j[1])),
)


def attend_tile(t, kv, qg, bias, gate, level_t, acc, res, level_sum):
    q_at = pl.ds(pl.multiple_of(t * TILE, TILE), TILE)
    k_at = pl.ds(pl.multiple_of(t * TILE, TILE), SLAB)
    k = kv[0, k_at, :]
    v = kv[1, k_at, :]
    q = qg[0, q_at, :]
    cot = qg[1, q_at, :].astype(F32)
    gate_rows = gate[q_at, :]
    g_t = (gate_rows * cot).astype(BF16).astype(F32).T
    z = mm(k, q, ((1,), (1,))) * (SCALE * LOG2E) + bias[t]
    top = jnp.max(z, axis=0, keepdims=True)
    e = jnp.exp2(z - top)
    inv = 1.0 / jnp.sum(e, axis=0, keepdims=True)
    e_low = e.astype(BF16)
    att_t = (mm(v, e_low, ((0,), (0,))) * inv).astype(BF16).astype(F32)
    dot = jnp.sum(g_t * att_t, axis=0, keepdims=True) * inv
    gs_t = (g_t * inv).astype(BF16)
    att = att_t.T
    d_prob = mm(v, gs_t)
    ds = (e * (d_prob - dot)).astype(BF16)
    acc[1, k_at, :] += mm(e_low, gs_t, ((1,), (1,)))
    acc[0, k_at, :] += mm(ds, q)
    dq_t = mm(k, ds, ((0,), (0,))) * SCALE
    res[0, q_at, :] = (gate_rows * att).astype(BF16)
    res[1, q_at, :] = dq_t.T.astype(BF16)
    prod = cot * att
    high = prod.astype(BF16)
    low = (prod - high.astype(F32)).astype(BF16)
    lev = level_t[:, q_at]
    level_sum[...] += mm(lev, high) + mm(lev, low)


def kernel(
    nz, span_ref, noise_ref, mask_ref, tab_ref, q_ref, k_ref, v_ref, c_ref,
    out_mq, out_kv, gate_buf,
    st_kv, st_qg, kv_a, kv_b, qg_a, qg_b, tab_a, tab_b, spans_t, spans_k, bias_a, bias_b, gate_a, gate_b, lev_a, lev_b,
    acc_a, acc_b, res_a, res_b, dkv_a, dkv_b, sb_a, sb_b, sa_a, sa_b, rb_a, rb_b, ra_a, ra_b,
    gate_part, gate_pair, gate_core, gate_all, pieces, sums, full, full_low,
    load_sem, in_send, in_recv, halo_send, halo_recv, part_send, part_recv, out_send, out_recv,
    gate_send, gate_recv,
):
    z, x, y, core = where_am_i()
    x_lo = lax.rem(x, 2)
    own_block = lax.div(x, 2) * 4 + y
    stays = core == x_lo
    pair_x = x + 1 - 2 * x_lo
    odd = lax.rem(z, 2)
    half = x_lo + odd - 2 * x_lo * odd
    piece = sums.shape[0]

    def remote(src, dst, send, recv, to):
        return pltpu.make_async_remote_copy(
            src_ref=src, dst_ref=dst, send_sem=send, recv_sem=recv, device_id=to, device_id_type=MESH
        )

    def took(ref, sem):
        pltpu.make_async_copy(ref, ref, sem).wait()

    def cols(head):
        return pl.ds(pl.multiple_of(head * DH, DH), DH)

    def rows(start, size):
        return pl.ds(pl.multiple_of(start, BLOCK), size)

    loads = [
        pltpu.make_async_copy(src, st.at[i], load_sem.at[n])
        for n, (src, st, i) in enumerate(
            ((k_ref, st_kv, 0), (v_ref, st_kv, 1), (q_ref, st_qg, 0), (c_ref, st_qg, 1))
        )
    ]
    loads += [
        pltpu.make_async_copy(tab_ref.at[:, cols(head)], tab, load_sem.at[n])
        for n, head, tab in ((4, whole_head(x, y), tab_a), (5, shared_head(x, y), tab_b))
    ]
    for load in loads:
        load.start()

    barrier = pltpu.get_barrier_semaphore()
    spot = x * 8 + y * 2 + core

    def greet_plane(j, carry):
        other = lax.rem(spot + j, 32)
        to = place(z, lax.div(other, 8), lax.rem(lax.div(other, 2), 4), lax.rem(other, 2))
        pl.semaphore_signal(barrier, inc=1, device_id=to, device_id_type=MESH)
        return carry

    lax.fori_loop(1, 32, greet_plane, 0)

    def greet_column(j, carry):
        to = place(lax.rem(z + j, nz), x, y, core)
        pl.semaphore_signal(barrier, inc=1, device_id=to, device_id_type=MESH)
        return carry

    lax.fori_loop(1, nz, greet_column, 0)
    beyond = lax.rem(z + nz - 1 + 2 * core, nz)
    pl.semaphore_signal(barrier, inc=1, device_id=place(beyond, x, y, 1 - core), device_id_type=MESH)
    pl.semaphore_wait(barrier, 31 + nz)

    def send_shared(st, dst, s):
        start = own_block * BLOCK
        at = dst.at[:, rows(WINDOW + start if dst is kv_b else start, BLOCK), :]
        for jx, jy in ((2, 2), (0, 2), (2, 1), (0, 3), (2, 3), (0, 1), (2, 0), (0, 0)):
            tx = lax.rem(x + jx + odd, 4)
            ty = lax.rem(y + jy, 4)
            src = st.at[:, :, cols(shared_head(tx, ty))]
            go = remote(src, at, in_send.at[s], in_recv.at[s], place(z, tx, ty, core))
            if (jx, jy) == (0, 0):
                @pl.when(odd == 0)
                def _():
                    pltpu.make_async_copy(src, at, in_recv.at[s]).start()

                @pl.when(odd == 1)
                def _():
                    go.start()
            else:
                go.start()

    def send_whole(st, dst, s, order=FAR_FIRST):
        start = core * WINDOW + own_block * BLOCK
        at = dst.at[:, rows(WINDOW + start if dst is kv_a else start, BLOCK), :]
        for jx, jy in order:
            tx = lax.rem(x + jx, 4)
            ty = lax.rem(y + jy, 4)
            src = st.at[:, :, cols(whole_head(tx, ty))]
            go = remote(src, at, in_send.at[s], in_recv.at[s], place(z, tx, ty, x_lo))
            if (jx, jy) == (0, 0):
                @pl.when(stays)
                def _():
                    pltpu.make_async_copy(src, at, in_recv.at[s]).start()

                @pl.when(jnp.logical_not(stays))
                def _():
                    go.start()
            else:
                go.start()

    loads[0].wait()
    loads[1].wait()
    send_shared(st_kv, kv_b, 0)
    loads[2].wait()
    loads[3].wait()
    send_shared(st_qg, qg_b, 1)

    loads[4].wait()
    loads[5].wait()
    start_a = z * PLANE + core * QA
    start_b = z * PLANE + (half * 2 + core) * QB
    prepare(start_b, span_ref, noise_ref, mask_ref, tab_b, spans_t, spans_k, bias_b, gate_b, lev_b)
    acc_b[...] = jnp.zeros_like(acc_b)
    gate_part[...] = jnp.zeros_like(gate_part)

    next_a = place(lax.rem(z + core, nz), x, y, 1 - core)
    prev_a = place(lax.rem(z + nz - 1 + core, nz), x, y, 1 - core)
    next_b = place(
        lax.rem(z + core * half, nz), jnp.where(core * (1 - half) == 1, pair_x, x), y, 1 - core
    )
    prev_b = place(
        lax.rem(z + nz - (1 - core) * (1 - half), nz),
        jnp.where((1 - core) * half == 1, pair_x, x),
        y,
        1 - core,
    )

    def halo(kv, queries, n, after, before):
        last = WINDOW + queries
        return (
            remote(
                kv.at[:, queries:last, :], kv.at[:, 0:WINDOW, :], halo_send.at[n], halo_recv.at[n], after
            ),
            remote(
                kv.at[:, WINDOW : WINDOW + SPAN, :],
                kv.at[:, last : last + SPAN, :],
                halo_send.at[n + 1],
                halo_recv.at[n + 1],
                before,
            ),
        )

    halo_b = halo(kv_b, QB, 0, next_b, prev_b)
    halo_a = halo(kv_a, QA, 2, next_a, prev_a)

    took(kv_b.at[:, WINDOW : WINDOW + QB, :], in_recv.at[0])
    for c in halo_b:
        c.start()
    send_whole(st_kv, kv_a, 2)
    prepare(start_a, span_ref, noise_ref, mask_ref, tab_a, spans_t, spans_k, bias_a, gate_a, lev_a)
    acc_a[...] = jnp.zeros_like(acc_a)
    took(qg_b, in_recv.at[1])
    send_whole(st_qg, qg_a, 3, FAR_FIRST[:8])
    for c in halo_b:
        c.wait()

    def give_shared(buf, out, i, s):
        src = buf.at[:, rows(i * BLOCK, BLOCK), :]
        dst = out.at[:, :, cols(shared_head(x, y))]
        mine = jnp.logical_and(odd == 0, i == own_block)

        @pl.when(mine)
        def _():
            pltpu.make_async_copy(src, dst, out_recv.at[s]).start()

        @pl.when(jnp.logical_not(mine))
        def _():
            to = place(z, lax.div(i, 4) * 2 + half, lax.rem(i, 4), core)
            remote(src, dst, out_send.at[s], out_recv.at[s], to).start()

    def give_whole(buf, out, i, s):
        src = buf.at[:, rows(i * BLOCK, BLOCK), :]
        dst = out.at[:, :, cols(whole_head(x, y))]
        mine = jnp.logical_and(stays, i == core * 8 + own_block)

        @pl.when(mine)
        def _():
            pltpu.make_async_copy(src, dst, out_recv.at[s]).start()

        @pl.when(jnp.logical_not(mine))
        def _():
            b = lax.rem(i, 8)
            to = place(z, lax.div(b, 4) * 2 + core, lax.rem(b, 4), lax.div(i, 8))
            remote(src, dst, out_send.at[2 + s], out_recv.at[s], to).start()

    turn = lax.div(own_block, 2) + 1

    def tile_b(step, carry):
        t = lax.rem(turn + step, QB // TILE)
        attend_tile(t, kv_b, qg_b, bias_b, gate_b, lev_b, acc_b, res_b, gate_part.at[1])
        return carry

    lax.fori_loop(0, QB // TILE, tile_b, 0)

    def part(buf, recv, n, to):
        return remote(buf, recv, part_send.at[n], part_recv.at[n], to)

    behind_b = part(sb_b, rb_b, 0, prev_b)
    ahead_b = part(sa_b, ra_b, 1, next_b)
    behind_a = part(sb_a, rb_a, 2, prev_a)
    ahead_a = part(sa_a, ra_a, 3, next_a)
    pair_gate = remote(
        gate_part.at[1], gate_pair, gate_send.at[0], gate_recv.at[0], place(z, pair_x, y, core)
    )

    for i, s in ((0, SCALE), (1, 1.0)):
        sb_b[i] = (acc_b[i, 0:WINDOW, :] * s).astype(BF16)
        sa_b[i] = (acc_b[i, WINDOW + QB :, :] * s).astype(BF16)
    took(kv_a.at[:, WINDOW : WINDOW + QA, :], in_recv.at[2])
    for c in halo_a:
        c.start()
    send_whole(st_qg, qg_a, 3, FAR_FIRST[8:])
    behind_b.start()
    ahead_b.start()
    pair_gate.start()

    def give_mixed(j, carry):
        give_shared(res_b, out_mq, lax.rem(own_block + 1 + j, QB // BLOCK), 0)
        return carry

    lax.fori_loop(0, QB // BLOCK, give_mixed, 0)
    took(qg_a, in_recv.at[3])
    for c in halo_a:
        c.wait()

    def finish_b():
        behind_b.wait()
        ahead_b.wait()
        for i, s in ((0, SCALE), (1, 1.0)):
            total = acc_b[i, WINDOW : WINDOW + QB, :] * s + rb_b[i].astype(F32)
            dkv_b[i] = total.astype(BF16)
            first = total[0:SPAN, :] + ra_b[i].astype(F32)
            dkv_b[i, 0:SPAN, :] = first.astype(BF16)

        def give(j, carry):
            give_shared(dkv_b, out_kv, lax.rem(own_block + 1 + j, QB // BLOCK), 1)
            return carry

        lax.fori_loop(0, QB // BLOCK, give, 0)

    def tile_a(step, carry):
        t = lax.div(step, 4) * 4 + lax.rem(turn + step, 4)
        attend_tile(t, kv_a, qg_a, bias_a, gate_a, lev_a, acc_a, res_a, gate_part.at[0])
        for j in range(TILE // BLOCK):
            give_whole(res_a, out_mq, t * (TILE // BLOCK) + j, 0)

        @pl.when(step == 1)
        def _():
            finish_b()

        @pl.when(step == 3)
        def _():
            for i, s in ((0, SCALE), (1, 1.0)):
                sb_a[i] = (acc_a[i, 0:WINDOW, :] * s).astype(BF16)
            behind_a.start()

        return carry

    lax.fori_loop(0, QA // TILE, tile_a, 0)

    for i, s in ((0, SCALE), (1, 1.0)):
        sa_a[i] = (acc_a[i, WINDOW + QA :, :] * s).astype(BF16)
    ahead_a.start()

    pair_gate.wait()
    gate_part[1] = gate_part[1] + gate_pair[...]
    other_core = place(z, x, y, 1 - core)
    core_gate = remote(
        gate_part.at[1 - core], gate_core, gate_send.at[1], gate_recv.at[1], other_core
    )
    core_gate.start()

    behind_a.wait()
    for i, s in ((0, SCALE), (1, 1.0)):
        own = acc_a[i, WINDOW + SPAN : 2 * WINDOW, :] * s
        dkv_a[i, SPAN:WINDOW, :] = own.astype(BF16)
        total = acc_a[i, 2 * WINDOW : 2 * WINDOW + WINDOW, :] * s + rb_a[i].astype(F32)
        dkv_a[i, WINDOW:, :] = total.astype(BF16)

    def give_rest(j, carry):
        i = lax.rem(core * 8 + own_block + 1 + j, QA // BLOCK)

        @pl.when(i >= SPAN // BLOCK)
        def _():
            give_whole(dkv_a, out_kv, i, 1)

        return carry

    core_gate.wait()
    gate_all[...] = gate_part[core] + gate_core[...]
    at_mine = pl.ds(pl.multiple_of(z * piece, piece), piece)

    def to_column(j, carry):
        other = lax.rem(z + j, nz)
        src = gate_all.at[pl.ds(pl.multiple_of(other * piece, piece), piece), :]
        to = place(other, x, y, core)
        remote(src, pieces.at[z], gate_send.at[2], gate_recv.at[2], to).start()
        return carry

    lax.fori_loop(1, nz, to_column, 0)
    lax.fori_loop(0, QA // BLOCK, give_rest, 0)

    took(pieces.at[0 : nz - 1], gate_recv.at[2])
    total = gate_all[at_mine, :]
    for j in range(1, nz):
        total = total + pieces[lax.rem(z + j, nz)]
    sums[...] = total
    full[at_mine, :] = total

    def back_to_column(j, carry):
        to = place(lax.rem(z + j, nz), x, y, core)
        remote(sums, full.at[at_mine, :], gate_send.at[3], gate_recv.at[3], to).start()
        return carry

    lax.fori_loop(1, nz, back_to_column, 0)

    ahead_a.wait()
    for i, s in ((0, SCALE), (1, 1.0)):
        first = acc_a[i, WINDOW : WINDOW + SPAN, :] * s + ra_a[i].astype(F32)
        dkv_a[i, 0:SPAN, :] = first.astype(BF16)
    def give_first(i, carry):
        give_whole(dkv_a, out_kv, i, 1)
        return carry

    lax.fori_loop(0, SPAN // BLOCK, give_first, 0)

    took(full.at[0 : (nz - 1) * piece, :], gate_recv.at[3])
    split = whole_head(0, 4) * DH
    half_rows = DH // 2
    low_rows = pl.ds(pl.multiple_of(x_lo * half_rows, half_rows), half_rows)
    row_a = pl.ds(pl.multiple_of(y * 4 * DH, DH), 4 * DH)
    row_b = pl.ds(pl.multiple_of(split + y * 2 * DH, DH), 2 * DH)
    full_low[...] = full[...].astype(BF16)

    def spread_gate(mine, row, one, three, all_rows, theirs):
        for jx in range(1, 4):
            to = place(z, lax.rem(x + jx, 4), y, core)
            remote(mine[0], mine[1], gate_send.at[4], gate_recv.at[4], to).start()
        took(one, gate_recv.at[4])
        for jy in range(1, 4):
            to = place(z, x, lax.rem(y + jy, 4), core)
            remote(row, row, gate_send.at[5], gate_recv.at[5], to).start()
        took(three, gate_recv.at[5])
        remote(all_rows, all_rows, gate_send.at[6], gate_recv.at[6], other_core).start()
        took(theirs, gate_recv.at[6])
        took(one, gate_send.at[4])
        took(three, gate_send.at[5])
        took(all_rows, gate_send.at[6])

    whole = gate_buf.at[:, 0:split]
    shared = gate_buf.at[:, split:]

    @pl.when(core == 0)
    def _():
        at = cols(whole_head(x, y))
        gate_buf[:, at] = full_low[...]
        spread_gate(
            (full_low, gate_buf.at[:, at]), gate_buf.at[:, row_a],
            gate_buf.at[:, 0 : 3 * DH], gate_buf.at[:, 0 : 12 * DH], whole, shared,
        )

    @pl.when(core == 1)
    def _():
        at = cols(shared_head(x, y))
        gate_buf[low_rows, at] = full_low[low_rows, :]
        spread_gate(
            (full_low.at[low_rows, :], gate_buf.at[low_rows, at]), gate_buf.at[:, row_b],
            gate_buf.at[0:half_rows, 0 : 3 * DH], gate_buf.at[:, 0 : 6 * DH], shared, whole,
        )

    took(pieces.at[0 : nz - 1], gate_send.at[2])
    took(full.at[0 : (nz - 1) * piece, :], gate_send.at[3])

    @pl.when(odd == 0)
    def _():
        for s in range(2):
            took(st_kv.at[:, :, 0 : 7 * DH], in_send.at[s])
            took(st_kv.at[:, :, 0 : 7 * DH], out_send.at[s])

    @pl.when(odd == 1)
    def _():
        for s in range(2):
            took(st_kv.at[:, :, 0 : 8 * DH], in_send.at[s])
            took(st_kv.at[:, :, 0 : 8 * DH], out_send.at[s])

    @pl.when(stays)
    def _():
        for s in range(2):
            took(st_kv.at[:, :, 0 : 15 * DH], in_send.at[2 + s])
            took(st_kv.at[:, :, 0 : 15 * DH], out_send.at[2 + s])

    @pl.when(jnp.logical_not(stays))
    def _():
        for s in range(2):
            took(st_kv.at[:, :, 0 : 16 * DH], in_send.at[2 + s])
            took(st_kv.at[:, :, 0 : 16 * DH], out_send.at[2 + s])

    took(out_mq, out_recv.at[0])
    took(out_kv, out_recv.at[1])


def fused(nz, span_rows, noise, mask, table, q, k, v, c):
    vmem = pl.BlockSpec(memory_space=pltpu.VMEM)
    hbm = pl.BlockSpec(memory_space=pl.ANY)
    block, width = q.shape
    spans = mask.shape[0]
    levels = table.shape[0]
    piece = levels // nz

    def low(*shape):
        return pltpu.VMEM(shape, BF16)

    def wide(*shape):
        return pltpu.VMEM(shape, F32)

    def sems(n):
        return pltpu.SemaphoreType.DMA((n,))

    rows_a, rows_b = QA + WINDOW + SPAN, QB + WINDOW + SPAN
    return pl.pallas_call(
        functools.partial(kernel, nz),
        out_shape=[
            jax.ShapeDtypeStruct((2, block, width), BF16),
            jax.ShapeDtypeStruct((2, block, width), BF16),
            jax.ShapeDtypeStruct((levels, width), BF16),
        ],
        in_specs=[vmem] * 3 + [hbm] * 5,
        out_specs=[hbm, hbm, vmem],
        scratch_shapes=[
            low(2, block, width), low(2, block, width),
            low(2, rows_a, DH), low(2, rows_b, DH), low(2, QA, DH), low(2, QB, DH),
            wide(levels, DH), wide(levels, DH),
            low(spans, rows_a), low(rows_a, spans),
            wide(QA // TILE, SLAB, TILE), wide(QB // TILE, SLAB, TILE),
            wide(QA, DH), wide(QB, DH), low(levels, QA), low(levels, QB),
            wide(2, rows_a, DH), wide(2, rows_b, DH),
            low(2, QA, DH), low(2, QB, DH), low(2, QA, DH), low(2, QB, DH),
            low(2, WINDOW, DH), low(2, WINDOW, DH), low(2, SPAN, DH), low(2, SPAN, DH),
            low(2, WINDOW, DH), low(2, WINDOW, DH), low(2, SPAN, DH), low(2, SPAN, DH),
            wide(2, levels, DH), wide(levels, DH), wide(levels, DH), wide(levels, DH),
            wide(nz, piece, DH), wide(piece, DH), wide(levels, DH), low(levels, DH),
            sems(6), sems(4), sems(4), sems(4), sems(4), sems(4), sems(4), sems(4), sems(2),
            sems(7), sems(7),
        ],
        compiler_params=pltpu.CompilerParams(
            collective_id=0, has_side_effects=True, vmem_limit_bytes=60 * 1024 * 1024
        ),
    )(span_rows, noise, mask, table, q, k, v, c)


def per_device(queries, key_rows, value_rows, out_cotangent, gate_table, span_ids, noise_level, block_mask):
    nz = lax.axis_size("ctx") // 4
    mq, kv, gate_low = fused(
        nz, span_ids.reshape(-1, BLOCK), noise_level[None, :], block_mask, gate_table,
        queries, key_rows, value_rows, out_cotangent,
    )
    return mq[0], mq[1], kv[0], kv[1], gate_low.astype(F32)


def solution(mesh):
    split = P(("ctx", "head"), None)
    return jax.shard_map(
        per_device,
        mesh=mesh,
        in_specs=(split, split, split, split, P(), P(), P(), P()),
        out_specs=(split, split, split, split, P()),
        check_vma=False,
    )
```

```python
import functools
import math

import jax
import jax.numpy as jnp
from jax import lax
from jax.experimental import pallas as pl
from jax.experimental.pallas import tpu as pltpu
from jax.sharding import PartitionSpec as P

DH = 128
SPAN = 256
WINDOW = 1024
TILE = 256
BLOCK = 128
SLAB = WINDOW + TILE + SPAN
QA = 2 * WINDOW
QB = WINDOW
PLANE = 4 * WINDOW
SCALE = 1.0 / math.sqrt(DH)
LOG2E = 1.0 / math.log(2.0)
HIDDEN = -1e30
F32 = jnp.float32
BF16 = jnp.bfloat16
MESH = pl.DeviceIdType.MESH


def mm(a, b, contract=((1,), (0,))):
    return lax.dot_general(a, b, (contract, ((), ())), preferred_element_type=F32)


def place(z, x, y, core):
    return (z * 4 + lax.rem(x, 2) * 2 + core, lax.div(x, 2) * 4 + y)


def where_am_i():
    ctx = lax.axis_index("ctx")
    head = lax.axis_index("head")
    z = lax.div(ctx, 4)
    x = lax.div(head, 4) * 2 + lax.rem(lax.div(ctx, 2), 2)
    return z, x, lax.rem(head, 4), lax.rem(ctx, 2)


def whole_head(x, y):
    return y * 4 + x


def shared_head(x, y):
    return 16 + y * 2 + lax.div(x, 2)


def prepare(start, span_ref, noise_ref, mask_ref, tab_ref, spans_t, spans_k, bias, gate, level_t):
    spans = mask_ref.shape[0]
    levels = tab_ref.shape[0]
    queries = bias.shape[0] * TILE
    rows = queries + WINDOW + SPAN
    total = span_ref.shape[0]
    first = lax.div(start, BLOCK) - WINDOW // BLOCK
    row = lax.broadcasted_iota(jnp.int32, (spans, BLOCK), 0)

    def encode(i, carry):
        block = first + i
        inside = jnp.logical_and(block >= 0, block < total)
        ids = span_ref[pl.ds(lax.rem(block + total, total), 1), :]
        onehot = (jnp.where(inside, ids, -1) == row).astype(F32)
        at = pl.ds(pl.multiple_of(i * BLOCK, BLOCK), BLOCK)
        spans_t[:, at] = onehot.astype(BF16)
        spans_k[at, :] = onehot.T.astype(BF16)
        return carry

    lax.fori_loop(0, rows // BLOCK, encode, 0)
    own = spans_t[:, WINDOW : WINDOW + queries]
    qs = lax.broadcasted_iota(jnp.int32, (spans, spans), 0)
    ks = lax.broadcasted_iota(jnp.int32, (spans, spans), 1)
    allowed = jnp.where(ks <= qs, mask_ref[...], 0).astype(F32).T.astype(BF16)
    mask_t = mm(allowed, own).astype(BF16)
    k_pos = lax.broadcasted_iota(jnp.int32, (TILE, TILE), 0)
    q_pos = lax.broadcasted_iota(jnp.int32, (TILE, TILE), 1)
    for t in range(bias.shape[0]):
        seen = mm(spans_k[t * TILE : t * TILE + SLAB, :], mask_t[:, t * TILE : (t + 1) * TILE])
        shown = jnp.where(seen > 0.5, 0.0, HIDDEN)
        bias[t, TILE:, :] = shown[TILE:, :]
        bias[t, 0:TILE, :] = jnp.where(k_pos > q_pos, shown[0:TILE, :], HIDDEN)
    lev = lax.broadcasted_iota(jnp.int32, (levels, spans), 0)
    span_level = (noise_ref[...] == lev).astype(BF16)
    level_t[...] = mm(span_level, own).astype(BF16)
    level = mm(spans_k[WINDOW : WINDOW + queries, :], span_level, ((1,), (1,))).astype(BF16)
    table = tab_ref[...]
    high = table.astype(BF16)
    low = (table - high.astype(F32)).astype(BF16)
    gate[...] = mm(level, high) + mm(level, low)


FAR_FIRST = sorted(
    ((jx, jy) for jy in range(4) for jx in range(4)),
    key=lambda j: -(min(j[0], 4 - j[0]) + min(j[1], 4 - j[1])),
)


HALO_STEP = 1


def attend_tile(t, kv, qg, bias, gate, level_t, acc, res, level_sum):
    q_at = pl.ds(pl.multiple_of(t * TILE, TILE), TILE)
    k_at = pl.ds(pl.multiple_of(t * TILE, TILE), SLAB)
    k = kv[0, k_at, :]
    v = kv[1, k_at, :]
    q = qg[0, q_at, :]
    cot = qg[1, q_at, :].astype(F32)
    gate_rows = gate[q_at, :]
    g_t = (gate_rows * cot).astype(BF16).astype(F32).T
    z = mm(k, q, ((1,), (1,))) * (SCALE * LOG2E) + bias[t]
    top = jnp.max(z, axis=0, keepdims=True)
    e = jnp.exp2(z - top)
    inv = 1.0 / jnp.sum(e, axis=0, keepdims=True)
    e_low = e.astype(BF16)
    att_t = (mm(v, e_low, ((0,), (0,))) * inv).astype(BF16).astype(F32)
    dot = jnp.sum(g_t * att_t, axis=0, keepdims=True) * inv
    gs_t = (g_t * inv).astype(BF16)
    att = att_t.T
    d_prob = mm(v, gs_t)
    ds = (e * (d_prob - dot)).astype(BF16)
    acc[1, k_at, :] += mm(e_low, gs_t, ((1,), (1,)))
    acc[0, k_at, :] += mm(ds, q)
    dq_t = mm(k, ds, ((0,), (0,))) * SCALE
    res[0, q_at, :] = (gate_rows * att).astype(BF16)
    res[1, q_at, :] = dq_t.T.astype(BF16)
    prod = cot * att
    high = prod.astype(BF16)
    low = (prod - high.astype(F32)).astype(BF16)
    lev = level_t[:, q_at]
    level_sum[...] += mm(lev, high) + mm(lev, low)


def forward_tile(t, kv, qg, bias, gate, level_t, res, level_sum, exps, scaled, dots):
    q_at = pl.ds(pl.multiple_of(t * TILE, TILE), TILE)
    k_at = pl.ds(pl.multiple_of(t * TILE, TILE), SLAB)
    cot = qg[1, q_at, :].astype(F32)
    gate_rows = gate[q_at, :]
    g_t = (gate_rows * cot).astype(BF16).astype(F32).T
    z = mm(kv[0, k_at, :], qg[0, q_at, :], ((1,), (1,))) * (SCALE * LOG2E) + bias[t]
    top = jnp.max(z, axis=0, keepdims=True)
    e = jnp.exp2(z - top)
    inv = 1.0 / jnp.sum(e, axis=0, keepdims=True)
    e_low = e.astype(BF16)
    exps[t] = e_low
    att_t = (mm(kv[1, k_at, :], e_low, ((0,), (0,))) * inv).astype(BF16).astype(F32)
    dots[t] = jnp.sum(g_t * att_t, axis=0, keepdims=True) * inv
    scaled[t] = (g_t * inv).astype(BF16)
    att = att_t.T
    res[0, q_at, :] = (gate_rows * att).astype(BF16)
    prod = cot * att
    high = prod.astype(BF16)
    low = (prod - high.astype(F32)).astype(BF16)
    lev = level_t[:, q_at]
    level_sum[...] += mm(lev, high) + mm(lev, low)


def backward_tile(t, kv, qg, acc, res, exps, scaled, dots):
    q_at = pl.ds(pl.multiple_of(t * TILE, TILE), TILE)
    k_at = pl.ds(pl.multiple_of(t * TILE, TILE), SLAB)
    e_low = exps[t]
    gs_t = scaled[t]
    d_prob = mm(kv[1, k_at, :], gs_t)
    ds = (e_low.astype(F32) * (d_prob - dots[t])).astype(BF16)
    acc[1, k_at, :] += mm(e_low, gs_t, ((1,), (1,)))
    acc[0, k_at, :] += mm(ds, qg[0, q_at, :])
    dq_t = mm(kv[0, k_at, :], ds, ((0,), (0,))) * SCALE
    res[1, q_at, :] = dq_t.T.astype(BF16)


def kernel(
    nz, span_ref, noise_ref, mask_ref, tab_ref, q_ref, k_ref, v_ref, c_ref,
    out_mq, out_kv, gate_buf,
    st_kv, st_qg, kv_a, kv_b, qg_a, qg_b, tab_a, tab_b, spans_t, spans_k, bias_a, bias_b, gate_a, gate_b, lev_a, lev_b,
    acc_a, acc_b, exps, scaled, dots, res_a, res_b, dkv_a, dkv_b, sb_a, sb_b, sa_a, sa_b, rb_a, rb_b, ra_a, ra_b,
    gate_part, gate_three, gate_core, gate_all, pieces, sums, full, full_low,
    load_sem, in_send, in_recv, halo_send, halo_recv, part_send, part_recv, out_send, out_recv,
    gate_send, gate_recv,
):
    z, x, y, core = where_am_i()
    x_lo = lax.rem(x, 2)
    own_block = lax.div(x, 2) * 4 + y
    stays = core == x_lo
    pair_x = x + 1 - 2 * x_lo
    odd = lax.rem(z, 2)
    half = x_lo + odd - 2 * x_lo * odd
    piece = sums.shape[0]

    def remote(src, dst, send, recv, to):
        return pltpu.make_async_remote_copy(
            src_ref=src, dst_ref=dst, send_sem=send, recv_sem=recv, device_id=to, device_id_type=MESH
        )

    def took(ref, sem):
        pltpu.make_async_copy(ref, ref, sem).wait()

    def cols(head):
        return pl.ds(pl.multiple_of(head * DH, DH), DH)

    def rows(start, size):
        return pl.ds(pl.multiple_of(start, BLOCK), size)

    loads = [
        pltpu.make_async_copy(src, st.at[i], load_sem.at[n])
        for n, (src, st, i) in enumerate(
            ((k_ref, st_kv, 0), (v_ref, st_kv, 1), (q_ref, st_qg, 0), (c_ref, st_qg, 1))
        )
    ]
    loads += [
        pltpu.make_async_copy(tab_ref.at[:, cols(head)], tab, load_sem.at[n])
        for n, head, tab in ((4, whole_head(x, y), tab_a), (5, shared_head(x, y), tab_b))
    ]
    for load in loads:
        load.start()

    barrier = pltpu.get_barrier_semaphore()
    spot = x * 8 + y * 2 + core

    def greet_plane(j, carry):
        other = lax.rem(spot + j, 32)
        to = place(z, lax.div(other, 8), lax.rem(lax.div(other, 2), 4), lax.rem(other, 2))
        pl.semaphore_signal(barrier, inc=1, device_id=to, device_id_type=MESH)
        return carry

    lax.fori_loop(1, 32, greet_plane, 0)

    def greet_column(j, carry):
        to = place(lax.rem(z + j, nz), x, y, core)
        pl.semaphore_signal(barrier, inc=1, device_id=to, device_id_type=MESH)
        return carry

    lax.fori_loop(1, nz, greet_column, 0)
    beyond = lax.rem(z + nz - 1 + 2 * core, nz)
    pl.semaphore_signal(barrier, inc=1, device_id=place(beyond, x, y, 1 - core), device_id_type=MESH)
    pl.semaphore_wait(barrier, 31 + nz)

    def send_shared(st, dst, s):
        start = own_block * BLOCK
        at = dst.at[:, rows(WINDOW + start if dst is kv_b else start, BLOCK), :]
        for jx, jy in ((2, 2), (0, 2), (2, 1), (0, 3), (2, 3), (0, 1), (2, 0), (0, 0)):
            tx = lax.rem(x + jx + odd, 4)
            ty = lax.rem(y + jy, 4)
            src = st.at[:, :, cols(shared_head(tx, ty))]
            go = remote(src, at, in_send.at[s], in_recv.at[s], place(z, tx, ty, core))
            if (jx, jy) == (0, 0):
                @pl.when(odd == 0)
                def _():
                    pltpu.make_async_copy(src, at, in_recv.at[s]).start()

                @pl.when(odd == 1)
                def _():
                    go.start()
            else:
                go.start()

    def send_whole(st, dst, s, order=FAR_FIRST):
        start = core * WINDOW + own_block * BLOCK
        at = dst.at[:, rows(WINDOW + start if dst is kv_a else start, BLOCK), :]
        for jx, jy in order:
            tx = lax.rem(x + jx, 4)
            ty = lax.rem(y + jy, 4)
            src = st.at[:, :, cols(whole_head(tx, ty))]
            go = remote(src, at, in_send.at[s], in_recv.at[s], place(z, tx, ty, x_lo))
            if (jx, jy) == (0, 0):
                @pl.when(stays)
                def _():
                    pltpu.make_async_copy(src, at, in_recv.at[s]).start()

                @pl.when(jnp.logical_not(stays))
                def _():
                    go.start()
            else:
                go.start()

    start_a = z * PLANE + core * QA
    start_b = z * PLANE + (half * 2 + core) * QB
    next_a = place(lax.rem(z + core, nz), x, y, 1 - core)
    prev_a = place(lax.rem(z + nz - 1 + core, nz), x, y, 1 - core)
    next_b = place(
        lax.rem(z + core * half, nz), jnp.where(core * (1 - half) == 1, pair_x, x), y, 1 - core
    )
    prev_b = place(
        lax.rem(z + nz - (1 - core) * (1 - half), nz),
        jnp.where((1 - core) * half == 1, pair_x, x),
        y,
        1 - core,
    )

    def halo(kv, queries, n, after, before):
        last = WINDOW + queries
        return (
            remote(
                kv.at[:, queries:last, :], kv.at[:, 0:WINDOW, :], halo_send.at[n], halo_recv.at[n], after
            ),
            remote(
                kv.at[:, WINDOW : WINDOW + SPAN, :],
                kv.at[:, last : last + SPAN, :],
                halo_send.at[n + 1],
                halo_recv.at[n + 1],
                before,
            ),
        )

    halo_b = halo(kv_b, QB, 0, next_b, prev_b)
    halo_a = halo(kv_a, QA, 2, next_a, prev_a)

    def give_shared(buf, out, i, s):
        src = buf.at[:, rows(i * BLOCK, BLOCK), :]
        dst = out.at[:, :, cols(shared_head(x, y))]
        mine = jnp.logical_and(odd == 0, i == own_block)

        @pl.when(mine)
        def _():
            pltpu.make_async_copy(src, dst, out_recv.at[s]).start()

        @pl.when(jnp.logical_not(mine))
        def _():
            to = place(z, lax.div(i, 4) * 2 + half, lax.rem(i, 4), core)
            remote(src, dst, out_send.at[s], out_recv.at[s], to).start()

    def give_whole(buf, out, i, s):
        src = buf.at[:, rows(i * BLOCK, BLOCK), :]
        dst = out.at[:, :, cols(whole_head(x, y))]
        mine = jnp.logical_and(stays, i == core * 8 + own_block)

        @pl.when(mine)
        def _():
            pltpu.make_async_copy(src, dst, out_recv.at[s]).start()

        @pl.when(jnp.logical_not(mine))
        def _():
            b = lax.rem(i, 8)
            to = place(z, lax.div(b, 4) * 2 + core, lax.rem(b, 4), lax.div(i, 8))
            remote(src, dst, out_send.at[2 + s], out_recv.at[s], to).start()

    def part(buf, recv, n, to):
        return remote(buf, recv, part_send.at[n], part_recv.at[n], to)

    behind_b = part(sb_b, rb_b, 0, prev_b)
    ahead_b = part(sa_b, ra_b, 1, next_b)
    behind_a = part(sb_a, rb_a, 2, prev_a)
    ahead_a = part(sa_a, ra_a, 3, next_a)
    def share_gate():
        def send(x_to, slot):
            to = place(z, x_to, y, 1)
            remote(
                gate_part.at[1], gate_three.at[slot], gate_send.at[0], gate_recv.at[0], to
            ).start()

        @pl.when(core == 0)
        def _():
            send(x, 0)
            send(pair_x, 1)

        @pl.when(core == 1)
        def _():
            send(pair_x, 2)

    def finish_b():
        behind_b.wait()
        ahead_b.wait()
        for i, s in ((0, SCALE), (1, 1.0)):
            total = acc_b[i, WINDOW : WINDOW + QB, :] * s + rb_b[i].astype(F32)
            dkv_b[i] = total.astype(BF16)
            first = total[0:SPAN, :] + ra_b[i].astype(F32)
            dkv_b[i, 0:SPAN, :] = first.astype(BF16)

        def give(j, carry):
            give_shared(dkv_b, out_kv, lax.rem(own_block + 1 + j, QB // BLOCK), 1)
            return carry

        lax.fori_loop(0, QB // BLOCK, give, 0)

    other_core = place(z, x, y, 1 - core)
    core_gate = remote(
        gate_part.at[0], gate_core, gate_send.at[1], gate_recv.at[1], other_core
    )
    at_mine = pl.ds(pl.multiple_of(z * piece, piece), piece)
    split = whole_head(0, 4) * DH
    half_rows = DH // 2
    low_rows = pl.ds(pl.multiple_of(x_lo * half_rows, half_rows), half_rows)
    at_a = cols(whole_head(x, y))
    at_b = cols(shared_head(x, y))
    whole = gate_buf.at[:, 0:split]
    shared = gate_buf.at[:, split:]
    along_x = (
        (full_low, gate_buf.at[:, at_a], gate_buf.at[:, 0 : 3 * DH]),
        (
            full_low.at[low_rows, :],
            gate_buf.at[low_rows, at_b],
            gate_buf.at[0:half_rows, 0 : 3 * DH],
        ),
    )
    along_y = (
        (gate_buf.at[:, pl.ds(pl.multiple_of(y * 4 * DH, DH), 4 * DH)], gate_buf.at[:, 0 : 12 * DH]),
        (
            gate_buf.at[:, pl.ds(pl.multiple_of(split + y * 2 * DH, DH), 2 * DH)],
            gate_buf.at[:, 0 : 6 * DH],
        ),
    )
    across = ((whole, shared), (shared, whole))


    def to_column(c):
        if c == 0:
            core_gate.wait_recv()
            gate_all[...] = gate_part[0] + gate_core[...]
        else:
            took(gate_three, gate_recv.at[0])
            gate_all[...] = gate_part[1] + gate_three[0] + gate_three[1] + gate_three[2]

        def send(j, carry):
            other = lax.rem(z + j, nz)
            src = gate_all.at[pl.ds(pl.multiple_of(other * piece, piece), piece), :]
            to = place(other, x, y, core)
            remote(src, pieces.at[z], gate_send.at[2], gate_recv.at[2], to).start()
            return carry

        lax.fori_loop(1, nz, send, 0)

    def back_to_column():
        took(pieces.at[0 : nz - 1], gate_recv.at[2])
        total = gate_all[at_mine, :]
        for j in range(1, nz):
            total = total + pieces[lax.rem(z + j, nz)]
        sums[...] = total
        full[at_mine, :] = total

        def send(j, carry):
            to = place(lax.rem(z + j, nz), x, y, core)
            remote(sums, full.at[at_mine, :], gate_send.at[3], gate_recv.at[3], to).start()
            return carry

        lax.fori_loop(1, nz, send, 0)

    def go_along_x(c):
        took(full.at[0 : (nz - 1) * piece, :], gate_recv.at[3])
        full_low[...] = full[...].astype(BF16)
        if c == 0:
            gate_buf[:, at_a] = full_low[...]
        else:
            gate_buf[low_rows, at_b] = full_low[low_rows, :]
        src, dst, _ = along_x[c]
        for jx in range(1, 4):
            to = place(z, lax.rem(x + jx, 4), y, core)
            remote(src, dst, gate_send.at[4], gate_recv.at[4], to).start()

    def go_along_y(c):
        took(along_x[c][2], gate_recv.at[4])
        mine = along_y[c][0]
        for jy in range(1, 4):
            to = place(z, x, lax.rem(y + jy, 4), core)
            remote(mine, mine, gate_send.at[5], gate_recv.at[5], to).start()

    def go_across(c):
        took(along_y[c][1], gate_recv.at[5])
        mine = across[c][0]
        remote(mine, mine, gate_send.at[6], gate_recv.at[6], other_core).start()

    def last(c):
        took(across[c][1], gate_recv.at[6])
        took(along_x[c][2], gate_send.at[4])
        took(along_y[c][1], gate_send.at[5])
        took(across[c][0], gate_send.at[6])
        took(gate_three.at[0 : 2 - c], gate_send.at[0])
        if c == 1:
            core_gate.wait_send()

    loads[0].wait()
    loads[1].wait()
    send_whole(st_kv, kv_a, 2)
    loads[2].wait()
    loads[3].wait()
    send_whole(st_qg, qg_a, 3, FAR_FIRST[:8])
    loads[4].wait()
    loads[5].wait()
    prepare(start_a, span_ref, noise_ref, mask_ref, tab_a, spans_t, spans_k, bias_a, gate_a, lev_a)
    acc_a[...] = jnp.zeros_like(acc_a)
    gate_part[...] = jnp.zeros_like(gate_part)
    took(kv_a.at[:, WINDOW : WINDOW + QA, :], in_recv.at[2])
    for c in halo_a:
        c.start()
    send_shared(st_kv, kv_b, 0)
    send_whole(st_qg, qg_a, 3, FAR_FIRST[8:])
    prepare(start_b, span_ref, noise_ref, mask_ref, tab_b, spans_t, spans_k, bias_b, gate_b, lev_b)
    acc_b[...] = jnp.zeros_like(acc_b)
    took(qg_a, in_recv.at[3])
    for c in halo_a:
        c.wait()
    send_shared(st_qg, qg_b, 1)

    turn = lax.div(own_block, 2) + 1

    def tile_a(step, carry):
        t = lax.div(step, 4) * 4 + lax.rem(turn + step, 4)
        attend_tile(t, kv_a, qg_a, bias_a, gate_a, lev_a, acc_a, res_a, gate_part.at[0])

        @pl.when(step == HALO_STEP)
        def _():
            took(kv_b.at[:, WINDOW : WINDOW + QB, :], in_recv.at[0])
            for c in halo_b:
                c.start()

        for j in range(TILE // BLOCK):
            give_whole(res_a, out_mq, t * (TILE // BLOCK) + j, 0)

        @pl.when(step == 3)
        def _():
            for i, s in ((0, SCALE), (1, 1.0)):
                sb_a[i] = (acc_a[i, 0:WINDOW, :] * s).astype(BF16)
            behind_a.start()

        return carry

    lax.fori_loop(0, QA // TILE, tile_a, 0)

    for i, s in ((0, SCALE), (1, 1.0)):
        sa_a[i] = (acc_a[i, WINDOW + QA :, :] * s).astype(BF16)
    ahead_a.start()

    @pl.when(core == 1)
    def _():
        core_gate.start()

    behind_a.wait()
    for i, s in ((0, SCALE), (1, 1.0)):
        own = acc_a[i, WINDOW + SPAN : 2 * WINDOW, :] * s
        dkv_a[i, SPAN:WINDOW, :] = own.astype(BF16)
        total = acc_a[i, 2 * WINDOW : 2 * WINDOW + WINDOW, :] * s + rb_a[i].astype(F32)
        dkv_a[i, WINDOW:, :] = total.astype(BF16)

    def give_rest(j, carry):
        i = lax.rem(core * 8 + own_block + 1 + j, QA // BLOCK)

        @pl.when(i >= SPAN // BLOCK)
        def _():
            give_whole(dkv_a, out_kv, i, 1)

        return carry

    lax.fori_loop(0, QA // BLOCK, give_rest, 0)
    took(qg_b, in_recv.at[1])
    for c in halo_b:
        c.wait()

    def forward_b(step, carry):
        t = lax.rem(turn + step, QB // TILE)
        forward_tile(
            t, kv_b, qg_b, bias_b, gate_b, lev_b, res_b, gate_part.at[1], exps, scaled, dots
        )

        @pl.when(jnp.logical_and(step == 0, core == 0))
        def _():
            to_column(0)

        @pl.when(jnp.logical_and(step == 3, core == 0))
        def _():
            back_to_column()

        return carry

    lax.fori_loop(0, QB // TILE, forward_b, 0)
    share_gate()

    def backward_b(step, carry):
        t = lax.rem(turn + step, QB // TILE)
        backward_tile(t, kv_b, qg_b, acc_b, res_b, exps, scaled, dots)

        @pl.when(jnp.logical_and(step == 0, core == 1))
        def _():
            to_column(1)

        @pl.when(jnp.logical_and(step == 2, core == 0))
        def _():
            go_along_x(0)

        @pl.when(step == 1)
        def _():
            ahead_a.wait()
            for i, s in ((0, SCALE), (1, 1.0)):
                first = acc_a[i, WINDOW : WINDOW + SPAN, :] * s + ra_a[i].astype(F32)
                dkv_a[i, 0:SPAN, :] = first.astype(BF16)

            def give_first(i, carry):
                give_whole(dkv_a, out_kv, i, 1)
                return carry

            lax.fori_loop(0, SPAN // BLOCK, give_first, 0)

        @pl.when(jnp.logical_and(step == 2, core == 1))
        def _():
            back_to_column()

        for j in range(TILE // BLOCK):
            give_shared(res_b, out_mq, t * (TILE // BLOCK) + j, 0)

        return carry

    lax.fori_loop(0, QB // TILE, backward_b, 0)

    for i, s in ((0, SCALE), (1, 1.0)):
        sb_b[i] = (acc_b[i, 0:WINDOW, :] * s).astype(BF16)
        sa_b[i] = (acc_b[i, WINDOW + QB :, :] * s).astype(BF16)
    behind_b.start()
    ahead_b.start()

    @pl.when(core == 0)
    def _():
        go_along_y(0)

    @pl.when(core == 1)
    def _():
        go_along_x(1)

    finish_b()

    @pl.when(core == 0)
    def _():
        go_across(0)

    @pl.when(core == 1)
    def _():
        go_along_y(1)

    @pl.when(core == 0)
    def _():
        last(0)

    @pl.when(core == 1)
    def _():
        go_across(1)
        last(1)

    took(pieces.at[0 : nz - 1], gate_send.at[2])
    took(full.at[0 : (nz - 1) * piece, :], gate_send.at[3])

    @pl.when(odd == 0)
    def _():
        for s in range(2):
            took(st_kv.at[:, :, 0 : 7 * DH], in_send.at[s])
            took(st_kv.at[:, :, 0 : 7 * DH], out_send.at[s])

    @pl.when(odd == 1)
    def _():
        for s in range(2):
            took(st_kv.at[:, :, 0 : 8 * DH], in_send.at[s])
            took(st_kv.at[:, :, 0 : 8 * DH], out_send.at[s])

    @pl.when(stays)
    def _():
        for s in range(2):
            took(st_kv.at[:, :, 0 : 15 * DH], in_send.at[2 + s])
            took(st_kv.at[:, :, 0 : 15 * DH], out_send.at[2 + s])

    @pl.when(jnp.logical_not(stays))
    def _():
        for s in range(2):
            took(st_kv.at[:, :, 0 : 16 * DH], in_send.at[2 + s])
            took(st_kv.at[:, :, 0 : 16 * DH], out_send.at[2 + s])

    took(out_mq, out_recv.at[0])
    took(out_kv, out_recv.at[1])


def fused(nz, span_rows, noise, mask, table, q, k, v, c):
    vmem = pl.BlockSpec(memory_space=pltpu.VMEM)
    hbm = pl.BlockSpec(memory_space=pl.ANY)
    block, width = q.shape
    spans = mask.shape[0]
    levels = table.shape[0]
    piece = levels // nz

    def low(*shape):
        return pltpu.VMEM(shape, BF16)

    def wide(*shape):
        return pltpu.VMEM(shape, F32)

    def sems(n):
        return pltpu.SemaphoreType.DMA((n,))

    rows_a, rows_b = QA + WINDOW + SPAN, QB + WINDOW + SPAN
    return pl.pallas_call(
        functools.partial(kernel, nz),
        out_shape=[
            jax.ShapeDtypeStruct((2, block, width), BF16),
            jax.ShapeDtypeStruct((2, block, width), BF16),
            jax.ShapeDtypeStruct((levels, width), BF16),
        ],
        in_specs=[vmem] * 3 + [hbm] * 5,
        out_specs=[hbm, hbm, vmem],
        scratch_shapes=[
            low(2, block, width), low(2, block, width),
            low(2, rows_a, DH), low(2, rows_b, DH), low(2, QA, DH), low(2, QB, DH),
            wide(levels, DH), wide(levels, DH),
            low(spans, rows_a), low(rows_a, spans),
            wide(QA // TILE, SLAB, TILE), wide(QB // TILE, SLAB, TILE),
            wide(QA, DH), wide(QB, DH), low(levels, QA), low(levels, QB),
            wide(2, rows_a, DH), wide(2, rows_b, DH),
            low(QB // TILE, SLAB, TILE), low(QB // TILE, DH, TILE), wide(QB // TILE, 1, TILE),
            low(2, QA, DH), low(2, QB, DH), low(2, QA, DH), low(2, QB, DH),
            low(2, WINDOW, DH), low(2, WINDOW, DH), low(2, SPAN, DH), low(2, SPAN, DH),
            low(2, WINDOW, DH), low(2, WINDOW, DH), low(2, SPAN, DH), low(2, SPAN, DH),
            wide(2, levels, DH), wide(3, levels, DH), wide(levels, DH), wide(levels, DH),
            wide(nz, piece, DH), wide(piece, DH), wide(levels, DH), low(levels, DH),
            sems(6), sems(4), sems(4), sems(4), sems(4), sems(4), sems(4), sems(4), sems(2),
            sems(7), sems(7),
        ],
        compiler_params=pltpu.CompilerParams(
            collective_id=0, has_side_effects=True, vmem_limit_bytes=60 * 1024 * 1024
        ),
    )(span_rows, noise, mask, table, q, k, v, c)


def per_device(queries, key_rows, value_rows, out_cotangent, gate_table, span_ids, noise_level, block_mask):
    nz = lax.axis_size("ctx") // 4
    mq, kv, gate_low = fused(
        nz, span_ids.reshape(-1, BLOCK), noise_level[None, :], block_mask, gate_table,
        queries, key_rows, value_rows, out_cotangent,
    )
    return mq[0], mq[1], kv[0], kv[1], gate_low.astype(F32)


def solution(mesh):
    split = P(("ctx", "head"), None)
    return jax.shard_map(
        per_device,
        mesh=mesh,
        in_specs=(split, split, split, split, P(), P(), P(), P()),
        out_specs=(split, split, split, split, P()),
        check_vma=False,
    )
```

```python
import functools
import math

import jax
import jax.numpy as jnp
from jax import lax
from jax.experimental import pallas as pl
from jax.experimental.pallas import tpu as pltpu
from jax.sharding import PartitionSpec as P

DH = 128
SPAN = 256
WINDOW = 1024
TILE = 256
BLOCK = 128
SLAB = WINDOW + TILE + SPAN
QA = 2 * WINDOW
QB = WINDOW
PLANE = 4 * WINDOW
SCALE = 1.0 / math.sqrt(DH)
LOG2E = 1.0 / math.log(2.0)
HIDDEN = -1e30
F32 = jnp.float32
BF16 = jnp.bfloat16
MESH = pl.DeviceIdType.MESH


def mm(a, b, contract=((1,), (0,))):
    return lax.dot_general(a, b, (contract, ((), ())), preferred_element_type=F32)


def place(z, x, y, core):
    return (z * 4 + lax.rem(x, 2) * 2 + core, lax.div(x, 2) * 4 + y)


def where_am_i():
    ctx = lax.axis_index("ctx")
    head = lax.axis_index("head")
    z = lax.div(ctx, 4)
    x = lax.div(head, 4) * 2 + lax.rem(lax.div(ctx, 2), 2)
    return z, x, lax.rem(head, 4), lax.rem(ctx, 2)


def whole_head(x, y):
    return y * 4 + x


def shared_head(x, y):
    return 16 + y * 2 + lax.div(x, 2)


def prepare(start, span_ref, noise_ref, mask_ref, tab_ref, spans_t, spans_k, bias, gate, level_t):
    spans = mask_ref.shape[0]
    levels = tab_ref.shape[0]
    queries = bias.shape[0] * TILE
    rows = queries + WINDOW + SPAN
    total = span_ref.shape[0]
    first = lax.div(start, BLOCK) - WINDOW // BLOCK
    row = lax.broadcasted_iota(jnp.int32, (spans, BLOCK), 0)

    def encode(i, carry):
        block = first + i
        inside = jnp.logical_and(block >= 0, block < total)
        ids = span_ref[pl.ds(lax.rem(block + total, total), 1), :]
        onehot = (jnp.where(inside, ids, -1) == row).astype(F32)
        at = pl.ds(pl.multiple_of(i * BLOCK, BLOCK), BLOCK)
        spans_t[:, at] = onehot.astype(BF16)
        spans_k[at, :] = onehot.T.astype(BF16)
        return carry

    lax.fori_loop(0, rows // BLOCK, encode, 0)
    own = spans_t[:, WINDOW : WINDOW + queries]
    qs = lax.broadcasted_iota(jnp.int32, (spans, spans), 0)
    ks = lax.broadcasted_iota(jnp.int32, (spans, spans), 1)
    allowed = jnp.where(ks <= qs, mask_ref[...], 0).astype(F32).T.astype(BF16)
    mask_t = mm(allowed, own).astype(BF16)
    k_pos = lax.broadcasted_iota(jnp.int32, (TILE, TILE), 0)
    q_pos = lax.broadcasted_iota(jnp.int32, (TILE, TILE), 1)
    for t in range(bias.shape[0]):
        seen = mm(spans_k[t * TILE : t * TILE + SLAB, :], mask_t[:, t * TILE : (t + 1) * TILE])
        shown = jnp.where(seen > 0.5, 0.0, HIDDEN)
        bias[t, TILE:, :] = shown[TILE:, :]
        bias[t, 0:TILE, :] = jnp.where(k_pos > q_pos, shown[0:TILE, :], HIDDEN)
    lev = lax.broadcasted_iota(jnp.int32, (levels, spans), 0)
    span_level = (noise_ref[...] == lev).astype(BF16)
    level_t[...] = mm(span_level, own).astype(BF16)
    level = mm(spans_k[WINDOW : WINDOW + queries, :], span_level, ((1,), (1,))).astype(BF16)
    table = tab_ref[...]
    high = table.astype(BF16)
    low = (table - high.astype(F32)).astype(BF16)
    gate[...] = mm(level, high) + mm(level, low)


FAR_FIRST = sorted(
    ((jx, jy) for jy in range(4) for jx in range(4)),
    key=lambda j: -(min(j[0], 4 - j[0]) + min(j[1], 4 - j[1])),
)


def attend_tile(t, kv, qg, bias, gate, level_t, acc, res, level_sum):
    q_at = pl.ds(pl.multiple_of(t * TILE, TILE), TILE)
    k_at = pl.ds(pl.multiple_of(t * TILE, TILE), SLAB)
    k = kv[0, k_at, :]
    v = kv[1, k_at, :]
    q = qg[0, q_at, :]
    cot = qg[1, q_at, :].astype(F32)
    gate_rows = gate[q_at, :]
    g_t = (gate_rows * cot).astype(BF16).astype(F32).T
    z = mm(k, q, ((1,), (1,))) * (SCALE * LOG2E) + bias[t]
    top = jnp.max(z, axis=0, keepdims=True)
    e = jnp.exp2(z - top)
    inv = 1.0 / jnp.sum(e, axis=0, keepdims=True)
    e_low = e.astype(BF16)
    att_t = (mm(v, e_low, ((0,), (0,))) * inv).astype(BF16).astype(F32)
    dot = jnp.sum(g_t * att_t, axis=0, keepdims=True) * inv
    gs_t = (g_t * inv).astype(BF16)
    att = att_t.T
    d_prob = mm(v, gs_t)
    ds = (e * (d_prob - dot)).astype(BF16)
    acc[1, k_at, :] += mm(e_low, gs_t, ((1,), (1,)))
    acc[0, k_at, :] += mm(ds, q)
    dq_t = mm(k, ds, ((0,), (0,))) * SCALE
    res[0, q_at, :] = (gate_rows * att).astype(BF16)
    res[1, q_at, :] = dq_t.T.astype(BF16)
    prod = cot * att
    high = prod.astype(BF16)
    low = (prod - high.astype(F32)).astype(BF16)
    lev = level_t[:, q_at]
    level_sum[...] += mm(lev, high) + mm(lev, low)


def kernel(
    nz, span_ref, noise_ref, mask_ref, tab_ref, q_ref, k_ref, v_ref, c_ref,
    out_mq, out_kv, gate_buf,
    st_kv, st_qg, kv_a, kv_b, qg_a, qg_b, tab_a, tab_b, spans_t, spans_k, bias_a, bias_b, gate_a, gate_b, lev_a, lev_b,
    acc_a, acc_b, res_a, res_b, dkv_a, dkv_b, sb_a, sb_b, sa_a, sa_b, rb_a, rb_b, ra_a, ra_b,
    gate_part, gate_pair, gate_core, gate_all, pieces, sums, full, full_low,
    load_sem, in_send, in_recv, halo_send, halo_recv, part_send, part_recv, out_send, out_recv,
    gate_send, gate_recv,
):
    z, x, y, core = where_am_i()
    x_lo = lax.rem(x, 2)
    own_block = lax.div(x, 2) * 4 + y
    stays = core == x_lo
    pair_x = x + 1 - 2 * x_lo
    odd = lax.rem(z, 2)
    half = x_lo + odd - 2 * x_lo * odd
    piece = sums.shape[0]

    def remote(src, dst, send, recv, to):
        return pltpu.make_async_remote_copy(
            src_ref=src, dst_ref=dst, send_sem=send, recv_sem=recv, device_id=to, device_id_type=MESH
        )

    def took(ref, sem):
        pltpu.make_async_copy(ref, ref, sem).wait()

    def cols(head):
        return pl.ds(pl.multiple_of(head * DH, DH), DH)

    def rows(start, size):
        return pl.ds(pl.multiple_of(start, BLOCK), size)

    loads = [
        pltpu.make_async_copy(src, st.at[i], load_sem.at[n])
        for n, (src, st, i) in enumerate(
            ((k_ref, st_kv, 0), (v_ref, st_kv, 1), (q_ref, st_qg, 0), (c_ref, st_qg, 1))
        )
    ]
    loads += [
        pltpu.make_async_copy(tab_ref.at[:, cols(head)], tab, load_sem.at[n])
        for n, head, tab in ((4, whole_head(x, y), tab_a), (5, shared_head(x, y), tab_b))
    ]
    for load in loads:
        load.start()

    barrier = pltpu.get_barrier_semaphore()
    spot = x * 8 + y * 2 + core

    def greet_plane(j, carry):
        other = lax.rem(spot + j, 32)
        to = place(z, lax.div(other, 8), lax.rem(lax.div(other, 2), 4), lax.rem(other, 2))
        pl.semaphore_signal(barrier, inc=1, device_id=to, device_id_type=MESH)
        return carry

    lax.fori_loop(1, 32, greet_plane, 0)

    def greet_column(j, carry):
        to = place(lax.rem(z + j, nz), x, y, core)
        pl.semaphore_signal(barrier, inc=1, device_id=to, device_id_type=MESH)
        return carry

    lax.fori_loop(1, nz, greet_column, 0)
    beyond = lax.rem(z + nz - 1 + 2 * core, nz)
    pl.semaphore_signal(barrier, inc=1, device_id=place(beyond, x, y, 1 - core), device_id_type=MESH)
    pl.semaphore_wait(barrier, 31 + nz)

    def send_shared(st, dst, s):
        start = own_block * BLOCK
        at = dst.at[:, rows(WINDOW + start if dst is kv_b else start, BLOCK), :]
        for jx, jy in ((2, 2), (0, 2), (2, 1), (0, 3), (2, 3), (0, 1), (2, 0), (0, 0)):
            tx = lax.rem(x + jx + odd, 4)
            ty = lax.rem(y + jy, 4)
            src = st.at[:, :, cols(shared_head(tx, ty))]
            go = remote(src, at, in_send.at[s], in_recv.at[s], place(z, tx, ty, core))
            if (jx, jy) == (0, 0):
                @pl.when(odd == 0)
                def _():
                    pltpu.make_async_copy(src, at, in_recv.at[s]).start()

                @pl.when(odd == 1)
                def _():
                    go.start()
            else:
                go.start()

    def send_whole(st, dst, s, order=FAR_FIRST):
        start = core * WINDOW + own_block * BLOCK
        at = dst.at[:, rows(WINDOW + start if dst is kv_a else start, BLOCK), :]
        for jx, jy in order:
            tx = lax.rem(x + jx, 4)
            ty = lax.rem(y + jy, 4)
            src = st.at[:, :, cols(whole_head(tx, ty))]
            go = remote(src, at, in_send.at[s], in_recv.at[s], place(z, tx, ty, x_lo))
            if (jx, jy) == (0, 0):
                @pl.when(stays)
                def _():
                    pltpu.make_async_copy(src, at, in_recv.at[s]).start()

                @pl.when(jnp.logical_not(stays))
                def _():
                    go.start()
            else:
                go.start()

    loads[0].wait()
    loads[1].wait()
    send_shared(st_kv, kv_b, 0)
    loads[2].wait()
    loads[3].wait()
    send_shared(st_qg, qg_b, 1)

    loads[4].wait()
    loads[5].wait()
    start_a = z * PLANE + core * QA
    start_b = z * PLANE + (half * 2 + core) * QB
    prepare(start_b, span_ref, noise_ref, mask_ref, tab_b, spans_t, spans_k, bias_b, gate_b, lev_b)
    acc_b[...] = jnp.zeros_like(acc_b)
    gate_part[...] = jnp.zeros_like(gate_part)

    next_a = place(lax.rem(z + core, nz), x, y, 1 - core)
    prev_a = place(lax.rem(z + nz - 1 + core, nz), x, y, 1 - core)
    next_b = place(
        lax.rem(z + core * half, nz), jnp.where(core * (1 - half) == 1, pair_x, x), y, 1 - core
    )
    prev_b = place(
        lax.rem(z + nz - (1 - core) * (1 - half), nz),
        jnp.where((1 - core) * half == 1, pair_x, x),
        y,
        1 - core,
    )

    def halo(kv, queries, n, after, before):
        last = WINDOW + queries
        return (
            remote(
                kv.at[:, queries:last, :], kv.at[:, 0:WINDOW, :], halo_send.at[n], halo_recv.at[n], after
            ),
            remote(
                kv.at[:, WINDOW : WINDOW + SPAN, :],
                kv.at[:, last : last + SPAN, :],
                halo_send.at[n + 1],
                halo_recv.at[n + 1],
                before,
            ),
        )

    halo_b = halo(kv_b, QB, 0, next_b, prev_b)
    halo_a = halo(kv_a, QA, 2, next_a, prev_a)

    took(kv_b.at[:, WINDOW : WINDOW + QB, :], in_recv.at[0])
    for c in halo_b:
        c.start()
    send_whole(st_kv, kv_a, 2)
    prepare(start_a, span_ref, noise_ref, mask_ref, tab_a, spans_t, spans_k, bias_a, gate_a, lev_a)
    acc_a[...] = jnp.zeros_like(acc_a)
    took(qg_b, in_recv.at[1])
    send_whole(st_qg, qg_a, 3, FAR_FIRST[:8])
    for c in halo_b:
        c.wait()

    def give_shared(buf, out, i, s):
        src = buf.at[:, rows(i * BLOCK, BLOCK), :]
        dst = out.at[:, :, cols(shared_head(x, y))]
        mine = jnp.logical_and(odd == 0, i == own_block)

        @pl.when(mine)
        def _():
            pltpu.make_async_copy(src, dst, out_recv.at[s]).start()

        @pl.when(jnp.logical_not(mine))
        def _():
            to = place(z, lax.div(i, 4) * 2 + half, lax.rem(i, 4), core)
            remote(src, dst, out_send.at[s], out_recv.at[s], to).start()

    def give_whole(buf, out, i, s):
        src = buf.at[:, rows(i * BLOCK, BLOCK), :]
        dst = out.at[:, :, cols(whole_head(x, y))]
        mine = jnp.logical_and(stays, i == core * 8 + own_block)

        @pl.when(mine)
        def _():
            pltpu.make_async_copy(src, dst, out_recv.at[s]).start()

        @pl.when(jnp.logical_not(mine))
        def _():
            b = lax.rem(i, 8)
            to = place(z, lax.div(b, 4) * 2 + core, lax.rem(b, 4), lax.div(i, 8))
            remote(src, dst, out_send.at[2 + s], out_recv.at[s], to).start()

    turn = lax.div(own_block, 2) + 1

    def tile_b(step, carry):
        t = lax.rem(turn + step, QB // TILE)
        attend_tile(t, kv_b, qg_b, bias_b, gate_b, lev_b, acc_b, res_b, gate_part.at[1])
        return carry

    lax.fori_loop(0, QB // TILE, tile_b, 0)

    def part(buf, recv, n, to):
        return remote(buf, recv, part_send.at[n], part_recv.at[n], to)

    behind_b = part(sb_b, rb_b, 0, prev_b)
    ahead_b = part(sa_b, ra_b, 1, next_b)
    behind_a = part(sb_a, rb_a, 2, prev_a)
    ahead_a = part(sa_a, ra_a, 3, next_a)
    pair_gate = remote(
        gate_part.at[1], gate_pair, gate_send.at[0], gate_recv.at[0], place(z, pair_x, y, core)
    )

    for i, s in ((0, SCALE), (1, 1.0)):
        sb_b[i] = (acc_b[i, 0:WINDOW, :] * s).astype(BF16)
        sa_b[i] = (acc_b[i, WINDOW + QB :, :] * s).astype(BF16)
    took(kv_a.at[:, WINDOW : WINDOW + QA, :], in_recv.at[2])
    for c in halo_a:
        c.start()
    send_whole(st_qg, qg_a, 3, FAR_FIRST[8:])
    behind_b.start()
    ahead_b.start()
    pair_gate.start()

    def give_mixed(j, carry):
        give_shared(res_b, out_mq, lax.rem(own_block + 1 + j, QB // BLOCK), 0)
        return carry

    lax.fori_loop(0, QB // BLOCK, give_mixed, 0)
    took(qg_a, in_recv.at[3])
    for c in halo_a:
        c.wait()

    def finish_b():
        behind_b.wait()
        ahead_b.wait()
        for i, s in ((0, SCALE), (1, 1.0)):
            total = acc_b[i, WINDOW : WINDOW + QB, :] * s + rb_b[i].astype(F32)
            dkv_b[i] = total.astype(BF16)
            first = total[0:SPAN, :] + ra_b[i].astype(F32)
            dkv_b[i, 0:SPAN, :] = first.astype(BF16)

        def give(j, carry):
            give_shared(dkv_b, out_kv, lax.rem(own_block + 1 + j, QB // BLOCK), 1)
            return carry

        lax.fori_loop(0, QB // BLOCK, give, 0)

    def tile_a(step, carry):
        t = lax.div(step, 4) * 4 + lax.rem(turn + step, 4)
        attend_tile(t, kv_a, qg_a, bias_a, gate_a, lev_a, acc_a, res_a, gate_part.at[0])
        for j in range(TILE // BLOCK):
            give_whole(res_a, out_mq, t * (TILE // BLOCK) + j, 0)

        @pl.when(step == 1)
        def _():
            finish_b()

        @pl.when(step == 3)
        def _():
            for i, s in ((0, SCALE), (1, 1.0)):
                sb_a[i] = (acc_a[i, 0:WINDOW, :] * s).astype(BF16)
            behind_a.start()

        return carry

    lax.fori_loop(0, QA // TILE, tile_a, 0)

    for i, s in ((0, SCALE), (1, 1.0)):
        sa_a[i] = (acc_a[i, WINDOW + QA :, :] * s).astype(BF16)
    ahead_a.start()

    pair_gate.wait()
    gate_part[1] = gate_part[1] + gate_pair[...]
    other_core = place(z, x, y, 1 - core)
    core_gate = remote(
        gate_part.at[1 - core], gate_core, gate_send.at[1], gate_recv.at[1], other_core
    )
    core_gate.start()

    behind_a.wait()
    for i, s in ((0, SCALE), (1, 1.0)):
        own = acc_a[i, WINDOW + SPAN : 2 * WINDOW, :] * s
        dkv_a[i, SPAN:WINDOW, :] = own.astype(BF16)
        total = acc_a[i, 2 * WINDOW : 2 * WINDOW + WINDOW, :] * s + rb_a[i].astype(F32)
        dkv_a[i, WINDOW:, :] = total.astype(BF16)

    def give_rest(j, carry):
        i = lax.rem(core * 8 + own_block + 1 + j, QA // BLOCK)

        @pl.when(i >= SPAN // BLOCK)
        def _():
            give_whole(dkv_a, out_kv, i, 1)

        return carry

    core_gate.wait()
    gate_all[...] = gate_part[core] + gate_core[...]
    at_mine = pl.ds(pl.multiple_of(z * piece, piece), piece)

    def to_column(j, carry):
        other = lax.rem(z + j, nz)
        src = gate_all.at[pl.ds(pl.multiple_of(other * piece, piece), piece), :]
        to = place(other, x, y, core)
        remote(src, pieces.at[z], gate_send.at[2], gate_recv.at[2], to).start()
        return carry

    lax.fori_loop(1, nz, to_column, 0)
    lax.fori_loop(0, QA // BLOCK, give_rest, 0)

    took(pieces.at[0 : nz - 1], gate_recv.at[2])
    total = gate_all[at_mine, :]
    for j in range(1, nz):
        total = total + pieces[lax.rem(z + j, nz)]
    sums[...] = total
    full[at_mine, :] = total

    def back_to_column(j, carry):
        to = place(lax.rem(z + j, nz), x, y, core)
        remote(sums, full.at[at_mine, :], gate_send.at[3], gate_recv.at[3], to).start()
        return carry

    lax.fori_loop(1, nz, back_to_column, 0)

    ahead_a.wait()
    for i, s in ((0, SCALE), (1, 1.0)):
        first = acc_a[i, WINDOW : WINDOW + SPAN, :] * s + ra_a[i].astype(F32)
        dkv_a[i, 0:SPAN, :] = first.astype(BF16)
    def give_first(i, carry):
        give_whole(dkv_a, out_kv, i, 1)
        return carry

    lax.fori_loop(0, SPAN // BLOCK, give_first, 0)

    took(full.at[0 : (nz - 1) * piece, :], gate_recv.at[3])
    split = whole_head(0, 4) * DH
    half_rows = DH // 2
    low_rows = pl.ds(pl.multiple_of(x_lo * half_rows, half_rows), half_rows)
    full_low[...] = full[...].astype(BF16)

    def spread_gate(src, dst, fifteen, mine, theirs):
        for jx, jy in FAR_FIRST[:-1]:
            to = place(z, lax.rem(x + jx, 4), lax.rem(y + jy, 4), core)
            remote(src, dst, gate_send.at[4], gate_recv.at[4], to).start()
        took(fifteen, gate_recv.at[4])
        remote(mine, mine, gate_send.at[6], gate_recv.at[6], other_core).start()
        took(theirs, gate_recv.at[6])
        took(fifteen, gate_send.at[4])
        took(mine, gate_send.at[6])

    whole = gate_buf.at[:, 0:split]
    shared = gate_buf.at[:, split:]

    @pl.when(core == 0)
    def _():
        at = cols(whole_head(x, y))
        gate_buf[:, at] = full_low[...]
        spread_gate(full_low, gate_buf.at[:, at], gate_buf.at[:, 0 : 15 * DH], whole, shared)

    @pl.when(core == 1)
    def _():
        at = cols(shared_head(x, y))
        gate_buf[low_rows, at] = full_low[low_rows, :]
        spread_gate(
            full_low.at[low_rows, :], gate_buf.at[low_rows, at],
            gate_buf.at[0:half_rows, 0 : 15 * DH], shared, whole,
        )

    took(pieces.at[0 : nz - 1], gate_send.at[2])
    took(full.at[0 : (nz - 1) * piece, :], gate_send.at[3])

    @pl.when(odd == 0)
    def _():
        for s in range(2):
            took(st_kv.at[:, :, 0 : 7 * DH], in_send.at[s])
            took(st_kv.at[:, :, 0 : 7 * DH], out_send.at[s])

    @pl.when(odd == 1)
    def _():
        for s in range(2):
            took(st_kv.at[:, :, 0 : 8 * DH], in_send.at[s])
            took(st_kv.at[:, :, 0 : 8 * DH], out_send.at[s])

    @pl.when(stays)
    def _():
        for s in range(2):
            took(st_kv.at[:, :, 0 : 15 * DH], in_send.at[2 + s])
            took(st_kv.at[:, :, 0 : 15 * DH], out_send.at[2 + s])

    @pl.when(jnp.logical_not(stays))
    def _():
        for s in range(2):
            took(st_kv.at[:, :, 0 : 16 * DH], in_send.at[2 + s])
            took(st_kv.at[:, :, 0 : 16 * DH], out_send.at[2 + s])

    took(out_mq, out_recv.at[0])
    took(out_kv, out_recv.at[1])


def fused(nz, span_rows, noise, mask, table, q, k, v, c):
    vmem = pl.BlockSpec(memory_space=pltpu.VMEM)
    hbm = pl.BlockSpec(memory_space=pl.ANY)
    block, width = q.shape
    spans = mask.shape[0]
    levels = table.shape[0]
    piece = levels // nz

    def low(*shape):
        return pltpu.VMEM(shape, BF16)

    def wide(*shape):
        return pltpu.VMEM(shape, F32)

    def sems(n):
        return pltpu.SemaphoreType.DMA((n,))

    rows_a, rows_b = QA + WINDOW + SPAN, QB + WINDOW + SPAN
    return pl.pallas_call(
        functools.partial(kernel, nz),
        out_shape=[
            jax.ShapeDtypeStruct((2, block, width), BF16),
            jax.ShapeDtypeStruct((2, block, width), BF16),
            jax.ShapeDtypeStruct((levels, width), BF16),
        ],
        in_specs=[vmem] * 3 + [hbm] * 5,
        out_specs=[hbm, hbm, vmem],
        scratch_shapes=[
            low(2, block, width), low(2, block, width),
            low(2, rows_a, DH), low(2, rows_b, DH), low(2, QA, DH), low(2, QB, DH),
            wide(levels, DH), wide(levels, DH),
            low(spans, rows_a), low(rows_a, spans),
            wide(QA // TILE, SLAB, TILE), wide(QB // TILE, SLAB, TILE),
            wide(QA, DH), wide(QB, DH), low(levels, QA), low(levels, QB),
            wide(2, rows_a, DH), wide(2, rows_b, DH),
            low(2, QA, DH), low(2, QB, DH), low(2, QA, DH), low(2, QB, DH),
            low(2, WINDOW, DH), low(2, WINDOW, DH), low(2, SPAN, DH), low(2, SPAN, DH),
            low(2, WINDOW, DH), low(2, WINDOW, DH), low(2, SPAN, DH), low(2, SPAN, DH),
            wide(2, levels, DH), wide(levels, DH), wide(levels, DH), wide(levels, DH),
            wide(nz, piece, DH), wide(piece, DH), wide(levels, DH), low(levels, DH),
            sems(6), sems(4), sems(4), sems(4), sems(4), sems(4), sems(4), sems(4), sems(2),
            sems(7), sems(7),
        ],
        compiler_params=pltpu.CompilerParams(
            collective_id=0, has_side_effects=True, vmem_limit_bytes=60 * 1024 * 1024
        ),
    )(span_rows, noise, mask, table, q, k, v, c)


def per_device(queries, key_rows, value_rows, out_cotangent, gate_table, span_ids, noise_level, block_mask):
    nz = lax.axis_size("ctx") // 4
    mq, kv, gate_low = fused(
        nz, span_ids.reshape(-1, BLOCK), noise_level[None, :], block_mask, gate_table,
        queries, key_rows, value_rows, out_cotangent,
    )
    return mq[0], mq[1], kv[0], kv[1], gate_low.astype(F32)


def solution(mesh):
    split = P(("ctx", "head"), None)
    return jax.shard_map(
        per_device,
        mesh=mesh,
        in_specs=(split, split, split, split, P(), P(), P(), P()),
        out_specs=(split, split, split, split, P()),
        check_vma=False,
    )
```
